256 devices in a mesh: section: 32 (over z_lo, y, core), expert: 8 (over x, z_hi).
Axes of the slice: x: 4, y: 4, z: 8 (z_hi: 2, z_lo: 4; z = z_hi * 4 + z_lo), core: 2. Of those that a mesh axis runs over, the one named last changes fastest.
Arguments:
- forward_in: bfloat16 [32, 512, 7168], P('section', 'expert'), may hold values from -6 to 6
- entering: bfloat16 [1, 512, 7168], P(None, 'expert'), may hold values from -6 to 6
- cotangent_in: bfloat16 [32, 512, 7168], P('section', 'expert'), may hold values from -6 to 6
- cot_entering: bfloat16 [1, 512, 7168], P(None, 'expert'), may hold values from -6 to 6
- stash: bfloat16 [2, 32, 512, 7168], P(None, 'section', 'expert'), may hold values from -6 to 6
- norm_gain: float32 [32, 7168], P('section'), may hold values from 0.5 to 1.5
- w_gate: bfloat16 [32, 1, 7168, 1024], P('section', None, None, 'expert'), may hold values from -0.0625 to 0.0625
- w_up: bfloat16 [32, 1, 7168, 1024], P('section', None, None, 'expert'), may hold values from -0.0625 to 0.0625
- w_down: bfloat16 [32, 1, 1024, 7168], P('section', None, 'expert'), may hold values from -0.1875 to 0.1875
- ids_fwd: int32 [2, 32, 512, 8], P(None, 'section'), may hold values from 0 to 255, as said below
- route_fwd: float32 [2, 32, 512, 8], P(None, 'section'), may hold values from 0.25 to 1.5
- ids_bwd: int32 [2, 32, 512, 8], P(None, 'section'), may hold values from 0 to 255, as said below
- route_bwd: float32 [2, 32, 512, 8], P(None, 'section'), may hold values from 0.25 to 1.5
Outputs:
- forward_out: bfloat16 [32, 512, 7168], P('section', 'expert')
- cotangent_out: bfloat16 [32, 512, 7168], P('section', 'expert')
The draws below stay inside these ranges and needn't reach their ends.
Inputs may be any that keep to these rules, and one draw needn't show every extreme that they name: `ids_fwd`: each row names 8 different experts. Among the 64 rows of one index of expert (aligned blocks of the token dimension), from 1 to 16 rows name any one expert below 1; for each such expert some step and layer have exactly 16 such rows on every index of expert. `ids_bwd`: as for ids_fwd.
All inputs are finite; a program needn't handle non-finite values.
Results may differ from the reference program's by a relative error of at most 0.006.
Values may be sent and summed in bfloat16 or wider, within the bound.
No kernel may reach another device: no remote copies, remote signals or barrier semaphores. Data moves between devices by JAX's collectives and lax.ppermute only.
A program may use at most 128 MiB of HBM per device.

```python
import jax
import jax.numpy as jnp
from jax import lax

D = 7168
FFE = 1024
EXPERTS = 256
TOPK = 8
FLIGHT = 1
TICKS = 2
TOK_DEV = 64
CAP = 16
TOK = 512
LAYERS = 32


def routed_ids(key):
    groups = TICKS * LAYERS
    blocks = TOK // TOK_DEV
    others = EXPERTS - FLIGHT
    keys = jax.random.split(key, 5)
    counts = jax.random.randint(keys[0], (groups, blocks, FLIGHT), 1, CAP + 1)
    full_at = jax.random.randint(keys[1], (FLIGHT,), 0, groups)
    group_ids = jnp.arange(groups, dtype=jnp.int32)
    counts = jnp.where(group_ids[:, None, None] == full_at[None, None, :], CAP, counts)
    scores = jax.random.randint(keys[2], (groups, blocks, TOK_DEV, FLIGHT), 0, 1 << 20)
    scores = scores * TOK_DEV + jnp.arange(TOK_DEV, dtype=jnp.int32)[None, None, :, None]
    order = jnp.argsort(scores, axis=2)
    ranks = jnp.argsort(order, axis=2)
    member = (ranks < counts[:, :, None, :]).reshape(groups, TOK, FLIGHT)
    other_scores = jax.random.randint(keys[3], (groups, TOK, others), 0, 1 << 20)
    other_scores = other_scores * others + jnp.arange(others, dtype=jnp.int32)[None, None, :]
    picked = lax.top_k(other_scores, TOPK)[1].astype(jnp.int32) + FLIGHT
    own_experts = jnp.arange(FLIGHT, dtype=jnp.int32)[None, None, :]
    candidates = jnp.concatenate([jnp.where(member, own_experts, -1), picked], axis=-1)
    valid = candidates >= 0
    position = jnp.cumsum(valid.astype(jnp.int32), axis=-1) - 1
    columns = jnp.arange(TOPK, dtype=jnp.int32)[None, None, None, :]
    chosen = valid[..., None] & (position[..., None] == columns)
    picked_ids = jnp.sum(jnp.where(chosen, candidates[..., None], 0), axis=2)
    shuffle = jax.random.randint(keys[4], (groups, TOK, TOPK), 0, 1 << 20)
    shuffle = shuffle * TOPK + jnp.arange(TOPK, dtype=jnp.int32)[None, None, :]
    permuted = jnp.argsort(shuffle, axis=-1)
    final_output = jnp.take_along_axis(picked_ids, permuted, axis=-1)
    return final_output.reshape(TICKS, LAYERS, TOK, TOPK).astype(jnp.int32)


def draw_ids_fwd(key, part):
    key = jax.random.fold_in(key, 11)
    return routed_ids(key)


def draw_ids_bwd(key, part):
    key = jax.random.fold_in(key, 23)
    return routed_ids(key)


def level_of(key, extent, pieces, least, largest):
    level, own = 1.0, jax.random.fold_in(key, 6)
    for dim, parts in pieces:
        draws = jnp.exp(jax.random.uniform(jax.random.fold_in(own, dim), (parts,), jnp.float32, least / len(pieces), largest / len(pieces)))
        level = level * jnp.repeat(draws, extent[dim] // parts).reshape([-1 if axis == dim else 1 for axis in range(len(extent))])
    return level


def scatter_about(own_key, extent, scale, limit, cuts=(), held_as=jnp.bfloat16):
    entries = jax.random.normal(own_key, extent, jnp.float32) * scale
    if len(cuts) > 0:
        entries = level_of(own_key, extent, cuts, -0.22, 0.18) * entries
    return jnp.clip(entries, min=-limit, max=limit).astype(held_as)


def setup_inputs(seed: int = 0) -> dict:
    key_list = jax.random.split(jax.random.key(seed), 14)
    forward_in = scatter_about(key_list[0], (LAYERS, TOK, D), 1.0, 6.0, ((0, 32), (1, 8)))
    entering = scatter_about(key_list[1], (TICKS - 1, TOK, D), 1.0, 6.0, ((1, 8),))
    cotangent_in = scatter_about(key_list[2], (LAYERS, TOK, D), 1.0, 6.0, ((0, 32), (1, 8)))
    cot_entering = scatter_about(key_list[3], (TICKS - 1, TOK, D), 1.0, 6.0, ((1, 8),))
    stash = scatter_about(key_list[4], (TICKS, LAYERS, TOK, D), 1.0, 6.0, ((1, 32), (2, 8)))
    norm_gain = jnp.clip(1.0 + 0.1 * jax.random.normal(key_list[5], (LAYERS, D), jnp.float32), 0.5, 1.5)
    w_gate = scatter_about(key_list[6], (LAYERS, FLIGHT, D, FFE), D ** -0.5, 0.0625, ((0, 32), (3, 8)))
    w_up = scatter_about(key_list[7], (LAYERS, FLIGHT, D, FFE), D ** -0.5, 0.0625, ((0, 32), (3, 8)))
    w_down = scatter_about(key_list[8], (LAYERS, FLIGHT, FFE, D), FFE ** -0.5, 0.1875, ((0, 32), (2, 8)))
    ids_fwd = draw_ids_fwd(jax.random.fold_in(key_list[13], 71), 0)
    route_fwd = jnp.clip(0.25 + 1.25 * jax.random.uniform(key_list[10], (TICKS, LAYERS, TOK, TOPK), jnp.float32) ** level_of(key_list[10], (TICKS, LAYERS, TOK, TOPK), ((1, 32),), -0.2, 0.2), 0.25, 1.5)
    ids_bwd = draw_ids_bwd(jax.random.fold_in(key_list[13], 71), 0)
    route_bwd = jnp.clip(0.25 + 1.25 * jax.random.uniform(key_list[12], (TICKS, LAYERS, TOK, TOPK), jnp.float32) ** level_of(key_list[12], (TICKS, LAYERS, TOK, TOPK), ((1, 32),), -0.2, 0.2), 0.25, 1.5)
    return {"forward_in": forward_in, "entering": entering, "cotangent_in": cotangent_in, "cot_entering": cot_entering, "stash": stash, "norm_gain": norm_gain, "w_gate": w_gate, "w_up": w_up, "w_down": w_down, "ids_fwd": ids_fwd, "route_fwd": route_fwd, "ids_bwd": ids_bwd, "route_bwd": route_bwd}


EPSILON = 1e-06

def routing(ids, weights):
    experts = jnp.arange(FLIGHT, dtype=jnp.int32)
    matches = (ids[:, :, None] == experts[None, None, :]).astype(jnp.float32)
    return lax.optimization_barrier(jnp.sum(weights[:, :, None] * matches, axis=1))

def norm_pieces(token_row_block, norm_scale):
    row_floats = token_row_block.astype(jnp.float32)
    inverse_root_square = lax.rsqrt(lax.optimization_barrier(jnp.mean(row_floats * row_floats, axis=-1, keepdims=True)) + EPSILON)
    centered_input = row_floats * inverse_root_square
    return ((centered_input * norm_scale).astype(jnp.bfloat16), centered_input, inverse_root_square)

def forward_layer(args):
    token_row_block, norm_scale, gate_w, up_w, down_w, ids, weights = args
    normalized_rows, centered_input, inverse_root_square = norm_pieces(token_row_block, norm_scale)
    gate_pre = jnp.einsum('rd,edf->erf', normalized_rows.astype(jnp.float32), gate_w.astype(jnp.float32))
    up_pre = jnp.einsum('rd,edf->erf', normalized_rows.astype(jnp.float32), up_w.astype(jnp.float32))
    hidden = (gate_pre * jax.nn.sigmoid(gate_pre) * up_pre).astype(jnp.bfloat16)
    outputs = jnp.einsum('erf,efd->erd', hidden.astype(jnp.float32), down_w.astype(jnp.float32))
    mix = routing(ids, weights)
    total = lax.optimization_barrier(jnp.sum(mix.T[:, :, None] * outputs, axis=0))
    return (token_row_block.astype(jnp.float32) + total).astype(jnp.bfloat16)

def backward_layer(args):
    token_row_block, upstream_gradient, norm_scale, gate_w, up_w, down_w, ids, weights = args
    normalized_rows, centered_input, inverse_root_square = norm_pieces(token_row_block, norm_scale)
    gate_pre = jnp.einsum('rd,edf->erf', normalized_rows.astype(jnp.float32), gate_w.astype(jnp.float32))
    up_pre = jnp.einsum('rd,edf->erf', normalized_rows.astype(jnp.float32), up_w.astype(jnp.float32))
    sigma = jax.nn.sigmoid(gate_pre)
    activated = gate_pre * sigma
    mix = routing(ids, weights)
    expert_cot = (mix.T[:, :, None] * upstream_gradient.astype(jnp.float32)[None]).astype(jnp.bfloat16)
    hidden_cot = jnp.einsum('erd,efd->erf', expert_cot.astype(jnp.float32), down_w.astype(jnp.float32))
    gate_cot = (hidden_cot * up_pre * sigma * (1.0 + gate_pre * (1.0 - sigma))).astype(jnp.bfloat16)
    up_cot = (hidden_cot * activated).astype(jnp.bfloat16)
    normed_cot = jnp.einsum('erf,edf->rd', gate_cot.astype(jnp.float32), gate_w.astype(jnp.float32))
    normed_cot = normed_cot + jnp.einsum('erf,edf->rd', up_cot.astype(jnp.float32), up_w.astype(jnp.float32))
    scaled_rows = normed_cot * norm_scale
    final_output = upstream_gradient.astype(jnp.float32) + inverse_root_square * (scaled_rows - centered_input * lax.optimization_barrier(jnp.mean(scaled_rows * centered_input, axis=-1, keepdims=True)))
    return final_output.astype(jnp.bfloat16)

def reference(forward_in, entering, cotangent_in, cot_entering, stash, norm_gain, w_gate, w_up, w_down, ids_fwd, route_fwd, ids_bwd, route_bwd):
    fwd_inputs = forward_in
    cot_inputs = cotangent_in
    forward_now = forward_in
    backward_now = cotangent_in
    for tick_index in range(TICKS):
        if tick_index > 0:
            fwd_inputs = jnp.concatenate([entering[tick_index - 1][None], forward_now[:-1]], axis=0)
            cot_inputs = jnp.concatenate([backward_now[1:], cot_entering[tick_index - 1][None]], axis=0)
        forward_now = lax.map(forward_layer, (fwd_inputs, norm_gain, w_gate, w_up, w_down, ids_fwd[tick_index], route_fwd[tick_index]))
        backward_now = lax.map(backward_layer, (stash[tick_index], cot_inputs, norm_gain, w_gate, w_up, w_down, ids_bwd[tick_index], route_bwd[tick_index]))
    return (forward_now, backward_now)
```

```python
import jax
import jax.numpy as jnp
from jax import lax
from jax.sharding import Mesh, PartitionSpec as P

CAP = 16
NX = 4
NZ = 2
EPSILON = 1e-06
BF = jnp.bfloat16
F32 = jnp.float32


def dot(a, b, contract=(1, 0)):
    dims = (((contract[0],), (contract[1],)), ((), ()))
    return lax.dot_general(a, b, dims, preferred_element_type=F32)


def to_x(block, distance):
    route = [(i, (i + distance) % NX) for i in range(NX)]
    return lax.ppermute(block, "x", route)


def to_other_z(block):
    return lax.ppermute(block, "zh", [(0, 1), (1, 0)])


def to_peer(block, distance, flip):
    route = []
    for x in range(NX):
        for z in range(NZ):
            route.append((x * NZ + z, ((x + distance) % NX) * NZ + (z ^ flip)))
    return lax.ppermute(block, ("x", "zh"), route)


def to_section(block, step, flip=0):
    count = lax.axis_size("section")
    route = []
    for s in range(count):
        if 0 <= s + step < count:
            for z in range(NZ):
                route.append((s * NZ + z, (s + step) * NZ + (z ^ flip)))
    return lax.ppermute(block, ("section", "zh"), route)


def routing_plans(ids, weights, zi):
    plans = ids.shape[0]
    matches = (ids == 0).astype(F32)
    mixing = jnp.sum(weights * matches, axis=-1).reshape(plans, NX, NZ, -1)
    member = jnp.sum(matches, axis=-1).reshape(plans, NX, NZ, -1)
    rows = member.shape[-1]
    swap = lambda a: jnp.where(zi == 0, a, a[:, :, ::-1])
    mixing = jnp.transpose(swap(mixing), (0, 2, 1, 3))
    member = jnp.transpose(swap(member), (0, 2, 1, 3))
    upto = (lax.broadcasted_iota(jnp.int32, (rows, rows), 0) <= lax.broadcasted_iota(jnp.int32, (rows, rows), 1)).astype(BF)
    order = dot(member.reshape(-1, rows).astype(BF), upto).reshape(member.shape)
    slot = jnp.where(member > 0, order, 0.0)
    wanted = jnp.arange(1, CAP + 1, dtype=jnp.int32).astype(F32)
    one_hot = (slot[..., None, :] == wanted[:, None]).astype(F32)
    slot_weight = jnp.sum(one_hot * mixing[..., None, :], axis=-1)
    return one_hot.astype(BF), slot_weight.reshape(plans, -1)


def by_x(pieces, xi):
    which = (xi - jnp.arange(NX)) % NX
    which = which.reshape((NX,) + (1,) * pieces[0].ndim)
    out = jnp.broadcast_to(pieces[0][None], (NX,) + pieces[0].shape)
    for d in range(1, NX):
        out = jnp.where(which == d, pieces[d][None], out)
    return out


def split_rows(packed, xi, width):
    pieces = []
    for d in range(NX):
        part = lax.dynamic_slice_in_dim(packed, ((xi + d) % NX) * width, width, 2)
        pieces.append(part if d == 0 else to_x(part, d))
    full = by_x(pieces, xi)
    return jnp.transpose(full, (1, 0, 2, 3)).reshape(packed.shape[0], NX * CAP, width)


def both_z(own):
    return jnp.concatenate([own, to_other_z(own)], axis=1)


def sum_over_x(partial, width):
    total = partial[:, :width]
    for d in range(1, NX):
        total = total + to_x(partial[:, d * width : (d + 1) * width].astype(BF), -d).astype(F32)
    return total


def all_sum_x(vector):
    total = vector
    for d in range(1, NX):
        total = total + to_x(vector, d)
    return total


def gather_x(block):
    return [block] + [to_x(block, d) for d in range(1, NX)]


def square_sum(rows):
    wide = rows.astype(F32)
    return jnp.sum(wide * wide, axis=-1)


def forward_hidden(pre, mix, half):
    gate, up = pre[:, :half], pre[:, half:]
    return (gate * jax.nn.sigmoid(gate) * up * mix[:, None]).astype(BF)


def rows_back(delta, xi):
    blocks = delta.reshape(NX, CAP, -1)
    pieces = []
    for d in range(NX):
        part = lax.dynamic_index_in_dim(blocks, (xi + d) % NX, 0, keepdims=False)
        pieces.append(part if d == 0 else to_x(part, d))
    full = by_x(pieces, xi)
    return jnp.transpose(full, (1, 0, 2)).reshape(CAP, -1)


def rows_back_both(delta, xi):
    blocks = delta.reshape(NZ, NX, CAP, -1)
    near, far = [], []
    for d in range(NX):
        part = lax.dynamic_index_in_dim(blocks, (xi + d) % NX, 1, keepdims=False)
        far.append(to_peer(part[1], d, 1))
        near.append(part[0] if d == 0 else to_peer(part[0], d, 0))
    pieces = [a.astype(F32) + b.astype(F32) for a, b in zip(near, far)]
    full = by_x(pieces, xi)
    return jnp.transpose(full, (1, 0, 2)).reshape(CAP, -1)


def on_device(
    forward_in,
    entering,
    cotangent_in,
    cot_entering,
    stash,
    norm_gain,
    w_gate,
    w_up,
    w_down,
    ids_fwd,
    route_fwd,
    ids_bwd,
    route_bwd,
):
    section = lax.axis_index("section")
    last = lax.axis_size("section") - 1
    xi = lax.axis_index("x")
    zi = lax.axis_index("zh")
    depth = stash.shape[-1]
    width = depth // NX
    half = w_gate.shape[-1]
    rows = NZ * NX * CAP

    ids = jnp.concatenate([ids_fwd[:, 0], ids_bwd[:, 0]], axis=0)
    routes = jnp.concatenate([route_fwd[:, 0], route_bwd[:, 0]], axis=0)
    hot, mix = routing_plans(ids, routes, zi)
    own = lax.dynamic_index_in_dim(hot[:, 0], xi, 1, keepdims=False)
    flat = hot.reshape(4, rows, -1)

    def pack(plan, source):
        return dot(own[plan], source).astype(BF)

    first = jnp.stack(
        [pack(0, forward_in[0]), pack(2, stash[0, 0]), pack(3, stash[1, 0]), pack(2, cotangent_in[0])]
    )
    first = both_z(split_rows(first, xi, width))
    stacked = first[:3].reshape(3 * rows, width)
    cot0 = first[3]

    gates, downs = [], []
    for d in range(NX):
        at = ((xi + d) % NX) * width
        pair = jnp.concatenate(
            [lax.dynamic_slice_in_dim(w[0, 0], at, width, 0) for w in (w_gate, w_up)], axis=1
        )
        gates.append(pair if d == 0 else to_x(pair, d))
    for d in range(NX):
        at = ((xi + d) % NX) * width
        part = lax.dynamic_slice_in_dim(w_down[0, 0], at, width, 1)
        downs.append(part if d == 0 else to_x(part, d))
    gate_up = jnp.concatenate(gates, axis=1)
    down = jnp.concatenate(downs, axis=0)
    gain = lax.dynamic_slice_in_dim(norm_gain[0], xi * width, width, 0)

    base_fwd = jnp.where(section == 0, entering[0], to_section(forward_in[0], 1))
    base_cot = jnp.where(section == last, cot_entering[0], to_section(cotangent_in[0], -1))
    hot_fwd = to_section(flat[0], 1)
    hot_cot = to_section(flat[2], -1)
    later = jnp.stack([pack(1, base_fwd), pack(3, base_cot)])
    later = both_z(split_rows(later, xi, width))

    group = jnp.arange(rows) // CAP
    same = (group[:, None] == group[None, :]).astype(F32)

    def carry(plan, before):
        move = (dot(flat[plan], before, (1, 1)) * same).astype(BF)
        return jnp.concatenate([move, jnp.roll(move, NX * CAP, axis=1)], axis=1)

    carry_fwd = carry(1, hot_fwd)
    carry_cot = carry(3, hot_cot)
    own_fwd0 = lax.dynamic_slice_in_dim(hot_fwd, xi * CAP, CAP, 0)
    own_cot0 = lax.dynamic_slice_in_dim(hot_cot, xi * CAP, CAP, 0)

    def inverse_rms(source):
        return lax.rsqrt(all_sum_x(square_sum(source)) / depth + EPSILON)

    def pre_activations(source, inverse):
        scaled = (source.astype(F32) * gain).astype(BF)
        return sum_over_x(dot(scaled, gate_up), 2 * half) * inverse[:, None]

    def ffn_out(hidden):
        return dot(jnp.concatenate(gather_x(hidden), axis=1), down).astype(BF)

    def backward(cot, pre, weight, source, inverse):
        hidden_cot = sum_over_x(dot(cot, down, (1, 1)), half) * weight[:, None]
        gate, up = pre[:, :half], pre[:, half:]
        sigma = jax.nn.sigmoid(gate)
        gate_cot = (hidden_cot * up * sigma * (1.0 + gate * (1.0 - sigma))).astype(BF)
        up_cot = (hidden_cot * gate * sigma).astype(BF)
        along = jnp.sum(gate_cot.astype(F32) * gate + up_cot.astype(F32) * up, axis=-1)
        along = all_sum_x(along) * inverse / depth
        pair = jnp.concatenate([gate_cot, up_cot], axis=1)
        normed_cot = dot(jnp.concatenate(gather_x(pair), axis=1), gate_up, (1, 1))
        return (
            inverse[:, None] * (normed_cot * gain - source.astype(F32) * along[:, None])
        ).astype(BF)

    inverse = inverse_rms(stacked)
    pre = pre_activations(stacked, inverse)
    pre_fwd0, pre_bwd = pre[:rows], [pre[rows : 2 * rows], pre[2 * rows :]]
    inv_bwd = [inverse[rows : 2 * rows], inverse[2 * rows :]]

    def step_on(delta, step):
        straight = to_section(delta, step)
        crossed = to_section(delta, step, 1)
        both = jnp.concatenate([straight, crossed], axis=0)
        done = straight[: NX * CAP].astype(F32) + crossed[NX * CAP :].astype(F32)
        return both, done.astype(BF)

    fwd_both, fwd_done = step_on(ffn_out(forward_hidden(pre_fwd0, mix[0], half)), 1)
    cot_both, cot_done = step_on(
        backward(cot0, pre_bwd[0], mix[2], first[1], inv_bwd[0]), -1
    )

    fwd1 = (later[0].astype(F32) + dot(carry_fwd, fwd_both)).astype(BF)
    fwd1_pre = pre_activations(fwd1, inverse_rms(fwd1))
    fwd1_out = ffn_out(forward_hidden(fwd1_pre, mix[1], half))
    cot1 = (later[1].astype(F32) + dot(carry_cot, cot_both)).astype(BF)
    cot1_out = backward(cot1, pre_bwd[1], mix[3], first[2], inv_bwd[1])

    def spread(hot_rows, delta):
        return dot(hot_rows, delta.astype(BF), (0, 0))

    fwd0_rows = (base_fwd.astype(F32) + spread(own_fwd0, rows_back(fwd_done, xi))).astype(BF)
    cot0_rows = (base_cot.astype(F32) + spread(own_cot0, rows_back(cot_done, xi))).astype(BF)
    fwd_out = fwd0_rows.astype(F32) + spread(own[1], rows_back_both(fwd1_out, xi))
    cot_out = cot0_rows.astype(F32) + spread(own[3], rows_back_both(cot1_out, xi))
    return (fwd_out.astype(BF)[None], cot_out.astype(BF)[None])


def solution(mesh):
    split = Mesh(mesh.devices.reshape(-1, NX, NZ), ("section", "x", "zh"))
    expert = ("x", "zh")
    placed = (
        P("section", expert, None),
        P(None, expert, None),
        P("section", expert, None),
        P(None, expert, None),
        P(None, "section", expert, None),
        P("section", None),
        P("section", None, None, expert),
        P("section", None, None, expert),
        P("section", None, expert, None),
        P(None, "section", None, None),
        P(None, "section", None, None),
        P(None, "section", None, None),
        P(None, "section", None, None),
    )
    return jax.shard_map(
        on_device,
        mesh=split,
        in_specs=placed,
        out_specs=(P("section", expert, None), P("section", expert, None)),
        check_vma=False,
    )
```

```python
import functools

import jax
import jax.numpy as jnp
from jax import lax
from jax.experimental import pallas as pl
from jax.experimental.pallas import tpu as pltpu
from jax.sharding import Mesh, PartitionSpec as P

CAP = 16
NX = 4
NZ = 2
EPSILON = 1e-06
BF = jnp.bfloat16
F32 = jnp.float32


def dot(a, b, contract=(1, 0)):
    dims = (((contract[0],), (contract[1],)), ((), ()))
    return lax.dot_general(a, b, dims, preferred_element_type=F32)


def to_x(block, distance):
    route = [(i, (i + distance) % NX) for i in range(NX)]
    return lax.ppermute(block, "x", route)


def to_other_z(block):
    return lax.ppermute(block, "zh", [(0, 1), (1, 0)])


def to_section(block, step, flip=0):
    count = lax.axis_size("section")
    route = []
    for s in range(count):
        if 0 <= s + step < count:
            for z in range(NZ):
                route.append((s * NZ + z, (s + step) * NZ + (z ^ flip)))
    return lax.ppermute(block, ("section", "zh"), route)


def routing_plans(ids, weights, zi):
    plans = ids.shape[0]
    matches = (ids == 0).astype(F32)
    mixing = jnp.sum(weights * matches, axis=-1).reshape(plans, NX, NZ, -1)
    member = jnp.sum(matches, axis=-1).reshape(plans, NX, NZ, -1)
    rows = member.shape[-1]
    swap = lambda a: jnp.where(zi == 0, a, a[:, :, ::-1])
    mixing = jnp.transpose(swap(mixing), (0, 2, 1, 3))
    member = jnp.transpose(swap(member), (0, 2, 1, 3))
    upto = (lax.broadcasted_iota(jnp.int32, (rows, rows), 0) <= lax.broadcasted_iota(jnp.int32, (rows, rows), 1)).astype(BF)
    order = dot(member.reshape(-1, rows).astype(BF), upto).reshape(member.shape)
    slot = jnp.where(member > 0, order, 0.0)
    wanted = jnp.arange(1, CAP + 1, dtype=jnp.int32).astype(F32)
    one_hot = (slot[..., None, :] == wanted[:, None]).astype(F32)
    spread = jnp.broadcast_to(mixing[..., None, :], one_hot.shape)
    slot_weight = jnp.sum((one_hot * spread).reshape(plans, -1, rows), axis=-1, keepdims=True)
    return one_hot.astype(BF), slot_weight


def after(value, *before):
    return lax.optimization_barrier((value,) + before)[0]


def two_words(column):
    high = lax.reduce_precision(column, 8, 7)
    low = column - high
    lane = lax.broadcasted_iota(jnp.int32, (column.shape[0], 128), 1)
    return jnp.where(lane == 0, high, jnp.where(lane == 1, low, 0.0)).astype(BF)


def kernel_call(kernel, outs, operands, flops=0, smem_first=False, scratch=()):
    specs = [pl.BlockSpec(memory_space=pltpu.VMEM) for _ in operands]
    if smem_first:
        specs[0] = pl.BlockSpec(memory_space=pltpu.SMEM)
    moved = sum(a.size * a.dtype.itemsize for a in list(operands) + list(outs))
    return pl.pallas_call(
        kernel,
        out_shape=outs,
        in_specs=specs,
        out_specs=[pl.BlockSpec(memory_space=pltpu.VMEM) for _ in outs],
        scratch_shapes=list(scratch),
        cost_estimate=pl.CostEstimate(flops=flops, bytes_accessed=moved, transcendentals=0),
        compiler_params=pltpu.CompilerParams(vmem_limit_bytes=24 * 2**20),
    )(*operands)


def shape(dims, dtype):
    return jax.ShapeDtypeStruct(dims, dtype)


def column_block(index, width):
    return pl.ds(pl.multiple_of(lax.rem(index, NX) * width, 128), width)


def pack_kernel(where, hot, fwd, stash, cot, *rest):
    outs, (hat1, word1, packed) = rest[:NX], rest[NX:]
    width = outs[0].shape[-1]
    x_fwd = dot(hot[0], fwd[...])
    x_bwd = dot(hot[2], stash[0])
    x_next = dot(hot[3], stash[1])
    g = dot(hot[2], cot[...])

    def inverse(x):
        return lax.rsqrt(jnp.mean(x * x, axis=-1, keepdims=True) + EPSILON)

    inv0, inv1 = inverse(x_bwd), inverse(x_next)
    packed[0] = (x_fwd * inverse(x_fwd)).astype(BF)
    packed[1] = (x_bwd * inv0).astype(BF)
    packed[2] = (g * inv0).astype(BF)
    hat1[...] = (x_next * inv1).astype(BF)
    word1[...] = jnp.broadcast_to(inv1, word1.shape)
    for d in range(NX):
        outs[d][...] = packed[:, :, column_block(where[0] + d, width)]


def pack_later_kernel(where, hot, fwd, cot, hat1, word1, *outs):
    *outs, packed = outs
    width = hat1.shape[-1] // NX
    inv1 = word1[:, :1]
    packed[0] = dot(hot[1], fwd[...]).astype(BF)
    packed[1] = (dot(hot[3], cot[...]) * inv1).astype(BF)
    packed[2] = hat1[...]
    words = two_words(inv1)
    for d in range(NX):
        outs[d][:, :, :width] = packed[:, :, column_block(where[0] + d, width)]
        for i in range(3):
            outs[d][i, :, width:] = words


def order_kernel(where, *refs):
    out = refs[NX]
    for d in range(NX):
        at = pl.multiple_of(lax.rem(where[0] + NX - d, NX) * CAP, CAP)
        out[:, pl.ds(at, CAP), :] = refs[d][...]


def both(own, other, index, width):
    return jnp.concatenate([own[index, :, :width], other[index, :, :width]], axis=0)


def pre_kernel(indices, own, other, gain, *refs):
    gates, outs = refs[:NX], refs[NX:]
    width = gain.shape[-1]
    for i, index in enumerate(indices):
        x = (both(own, other, index, width).astype(F32) * gain[...]).astype(BF)
        for w, out in zip(gates, outs):
            out[i * x.shape[0] : (i + 1) * x.shape[0], :] = dot(x, w[...]).astype(out.dtype)


def pre_next_kernel(own, other, gain, carry, straight, crossed, *refs):
    gates, outs = refs[:NX], refs[NX:]
    width, half = gain.shape[-1], gates[0].shape[-1]
    count = straight.shape[0]
    x = both(own, other, 0, width).astype(F32)
    x = x + dot(carry[:, :count], straight[...]) + dot(carry[:, count:], crossed[...])
    squares = jnp.sum(x * x, axis=-1, keepdims=True)
    x = (x * gain[...]).astype(BF)
    for d in range(NX):
        outs[d][:, :half] = dot(x, gates[d][...]).astype(outs[d].dtype)
        outs[d][:, half:] = two_words(squares).astype(outs[d].dtype)


def cot_kernel(own, other, *refs):
    downs, outs = refs[:NX], refs[NX:]
    x = both(own, other, 2, own.shape[-1])
    for w, out in zip(downs, outs):
        out[...] = dot(x, w[...], (1, 1)).astype(out.dtype)


def cot_next_kernel(own, other, carry, straight, crossed, *refs):
    downs, outs = refs[:NX], refs[NX:]
    width, count = straight.shape[-1], straight.shape[0]
    words = jnp.concatenate([own[2, :, width:], other[2, :, width:]], axis=0).astype(F32)
    inverse = words[:, :1] + words[:, 1:2]
    moved = dot(carry[:, :count], straight[...]) + dot(carry[:, count:], crossed[...])
    x = (both(own, other, 1, width).astype(F32) + inverse * moved).astype(BF)
    for w, out in zip(downs, outs):
        out[...] = dot(x, w[...], (1, 1)).astype(out.dtype)


def total(parts, rows=slice(None), columns=slice(None)):
    return sum(p[rows, columns].astype(F32) for p in parts)


def hidden_kernel(depth, mix, *refs):
    parts, out = refs[:NX], refs[NX]
    count, half = out.shape
    gate = total(parts, slice(0, count), slice(0, half))
    up = total(parts, slice(0, count), slice(half, 2 * half))
    if parts[0].shape[1] > 2 * half:
        words = total(parts, slice(0, count), slice(2 * half, None))
        scale = lax.rsqrt((words[:, :1] + words[:, 1:2]) / depth + EPSILON)
        gate, up = gate * scale, up * scale
    out[...] = (gate * jax.nn.sigmoid(gate) * up * mix[...]).astype(BF)


def pair_kernel(start, mix, *refs):
    cots, parts, out = refs[:NX], refs[NX : 2 * NX], refs[2 * NX]
    count, half = cots[0].shape
    rows = slice(start, start + count)
    hidden_cot = total(cots) * mix[...]
    gate = total(parts, rows, slice(0, half))
    up = total(parts, rows, slice(half, 2 * half))
    sigma = jax.nn.sigmoid(gate)
    gate_cot = hidden_cot * up * sigma * (1.0 + gate * (1.0 - sigma))
    up_cot = hidden_cot * gate * sigma
    out[:, :half] = gate_cot.astype(BF)
    out[:, half : 2 * half] = up_cot.astype(BF)
    out[:, 2 * half :] = (gate_cot * gate + up_cot * up).astype(BF)


def put(outs, value):
    at = 0
    for out in outs:
        out[...] = value[at : at + out.shape[0]].astype(out.dtype)
        at += out.shape[0]


def ffn_kernel(*refs):
    hidden, downs, outs = refs[:NX], refs[NX : 2 * NX], refs[2 * NX :]
    put(outs, sum(dot(h[...], w[...]) for h, w in zip(hidden, downs)))


def cot_out_kernel(index, own, other, gain, *refs):
    pairs, gates, outs = refs[:NX], refs[NX : 2 * NX], refs[2 * NX :]
    width, wide = gain.shape[-1], gates[0].shape[-1]
    normed_cot = sum(dot(p[:, :wide], w[...], (1, 1)) for p, w in zip(pairs, gates))
    along = total(pairs, slice(None), slice(wide, None))
    along = jnp.sum(along, axis=-1, keepdims=True) / (NX * width)
    hat = both(own, other, index, width).astype(F32)
    put(outs, normed_cot * gain[...] - hat * along)


def final_kernel(where, base, hot0, hot1, *refs):
    before, now, out = refs[:NX], refs[NX : 2 * NX], refs[2 * NX]
    width = before[0].shape[-1]
    for d in range(NX):
        at = column_block(where[0] + NX - d, width)
        rows = base[:, at].astype(F32) + dot(hot0[...], before[d][...], (0, 0))
        rows = rows.astype(BF).astype(F32) + dot(hot1[...], now[d][...], (0, 0))
        out[:, at] = rows.astype(BF)


def back_x(delta, xi):
    pieces = []
    for d in range(NX):
        part = lax.dynamic_slice_in_dim(delta, ((xi + d) % NX) * CAP, CAP, 0)
        pieces.append(part if d == 0 else to_x(part, d))
    return pieces


def gather_x(block):
    return [block] + [to_x(block, d) for d in range(1, NX)]


def sum_parts(parts):
    return [parts[0]] + [to_x(parts[d], -d) for d in range(1, NX)]


def on_device(
    forward_in,
    entering,
    cotangent_in,
    cot_entering,
    stash,
    norm_gain,
    w_gate,
    w_up,
    w_down,
    ids_fwd,
    route_fwd,
    ids_bwd,
    route_bwd,
):
    section = lax.axis_index("section")
    last = lax.axis_size("section") - 1
    xi = lax.axis_index("x")
    zi = lax.axis_index("zh")
    depth = stash.shape[-1]
    width = depth // NX
    half = w_gate.shape[-1]
    rows = NZ * NX * CAP

    ids = jnp.concatenate([ids_fwd[:, 0], ids_bwd[:, 0]], axis=0)
    routes = jnp.concatenate([route_fwd[:, 0], route_bwd[:, 0]], axis=0)
    hot, mix = routing_plans(ids, routes, zi)
    own = lax.dynamic_index_in_dim(hot[:, 0], xi, 1, keepdims=False)
    flat = hot.reshape(4, rows, -1)

    where = xi.astype(jnp.int32).reshape(1)

    wide = [shape((3, CAP, width), BF)] * NX
    *first, hat1, word1 = kernel_call(
        pack_kernel,
        wide + [shape((CAP, depth), BF), shape((CAP, 128), F32)],
        [where, own, forward_in[0], stash[:, 0], cotangent_in[0]],
        smem_first=True,
        scratch=[pltpu.VMEM((3, CAP, depth), BF)],
    )
    first = [first[0]] + [to_x(first[d], d) for d in range(1, NX)]

    moved_fwd = to_section(forward_in[0], 1)
    moved_cot = to_section(cotangent_in[0], -1)
    hot_fwd = to_section(flat[0], 1)
    hot_cot = to_section(flat[2], -1)

    def gate_up_part(d):
        at = ((xi + d) % NX) * width
        return jnp.concatenate(
            [lax.dynamic_slice_in_dim(w[0, 0], at, width, 0) for w in (w_gate, w_up)], axis=1
        )

    def down_part(d):
        return lax.dynamic_slice_in_dim(w_down[0, 0], ((xi + d) % NX) * width, width, 1)

    gates = [gate_up_part(0), to_x(gate_up_part(1), 1), None, to_x(gate_up_part(3), 3)]
    gates[2] = to_x(after(gate_up_part(2), *first[1:]), 2)
    downs = [down_part(0)] + [to_x(after(down_part(d), gates[2]), d) for d in range(1, NX)]
    gain = lax.dynamic_slice_in_dim(norm_gain, xi * width, width, 1)

    def in_order(pieces):
        count, _, columns = pieces[0].shape
        out = [shape((count, NX * CAP, columns), BF)]
        return kernel_call(order_kernel, out, [where] + pieces, smem_first=True)[0]

    first_own = in_order(first)
    first_other = to_other_z(first_own)

    base_fwd = jnp.where(section == 0, entering[0], moved_fwd)
    base_cot = jnp.where(section == last, cot_entering[0], moved_cot)
    later = kernel_call(
        pack_later_kernel,
        [shape((3, CAP, width + 128), BF)] * NX,
        [where, own, base_fwd, base_cot, hat1, word1],
        smem_first=True,
        scratch=[pltpu.VMEM((3, CAP, depth), BF)],
    )
    later = [later[0]] + [to_x(after(later[d], gates[1], gates[3]), d) for d in range(1, NX)]
    later_own = in_order(later)
    later_other = to_other_z(after(later_own, first_other))

    group = jnp.arange(rows) // CAP
    same = (group[:, None] == group[None, :]).astype(F32)

    def carry(plan, before):
        move = (dot(flat[plan], before, (1, 1)) * same).astype(BF)
        return jnp.concatenate([move, jnp.roll(move, NX * CAP, axis=1)], axis=1)

    carry_fwd = carry(1, hot_fwd)
    carry_cot = carry(3, hot_cot)
    own_fwd0 = lax.dynamic_slice_in_dim(hot_fwd, xi * CAP, CAP, 0)
    own_cot0 = lax.dynamic_slice_in_dim(hot_cot, xi * CAP, CAP, 0)

    product = 2 * rows * width * half

    def parts_of(kernel, operands, columns, count, terms):
        outs = [shape((count, columns), F32)] + [shape((count, columns), BF)] * (NX - 1)
        return kernel_call(kernel, outs, operands, flops=terms * NX * product)

    whole = [shape((rows, width), BF)]
    halves = [shape((NX * CAP, width), BF)] * 2

    def ffn_out(mixing, parts, outs):
        hidden = kernel_call(functools.partial(hidden_kernel, depth), [shape((rows, half), BF)], [mixing] + parts)[0]
        return kernel_call(ffn_kernel, outs, gather_x(hidden) + downs, flops=NX * product)

    def cot_out(pair, own_rows, other_rows, index, outs):
        return kernel_call(
            functools.partial(cot_out_kernel, index),
            outs,
            [own_rows, other_rows, gain] + gather_x(pair) + gates,
            flops=2 * NX * product,
        )

    def pair_of(start, mixing, cots, parts):
        out = [shape((rows, 3 * half), BF)]
        return kernel_call(functools.partial(pair_kernel, start), out, [mixing] + cots + parts)[0]

    pre = sum_parts(
        parts_of(
            functools.partial(pre_kernel, (0, 1)),
            [first_own, first_other, gain] + gates,
            2 * half,
            2 * rows,
            4,
        )
    )
    fwd0 = ffn_out(mix[0], pre, whole)[0]
    cots0 = sum_parts(parts_of(cot_kernel, [first_own, first_other] + downs, half, rows, 1))
    fwd_straight = to_section(fwd0, 1)
    fwd_crossed = to_section(fwd0, 1, 1)
    pair0 = pair_of(rows, mix[2], [after(cots0[0], fwd0)] + cots0[1:], pre)
    cot0 = cot_out(pair0, first_own, first_other, 1, whole)[0]
    cot_straight = to_section(cot0, -1)
    cot_crossed = to_section(cot0, -1, 1)

    pre1 = sum_parts(
        parts_of(
            functools.partial(pre_kernel, (2,)),
            [after(later_own, cot0), later_other, gain] + gates,
            2 * half,
            rows,
            2,
        )
    )
    next_pre = sum_parts(
        parts_of(
            pre_next_kernel,
            [later_own, later_other, gain, carry_fwd, fwd_straight, fwd_crossed] + gates,
            3 * half,
            rows,
            2,
        )
    )
    fwd1 = ffn_out(mix[1], next_pre, halves)
    cots1 = sum_parts(
        parts_of(
            cot_next_kernel,
            [later_own, later_other, carry_cot, after(cot_straight, fwd_straight), cot_crossed] + downs,
            half,
            rows,
            1,
        )
    )
    pair1 = pair_of(0, mix[3], [after(cots1[0], fwd1[0])] + cots1[1:], pre1)
    cot1 = cot_out(pair1, later_own, later_other, 2, halves)

    def add_half(a, b):
        return (a.astype(F32) + b.astype(F32)).astype(BF)

    def finish(base, hot0, hot1, straight, crossed, now):
        count = NX * CAP
        before = back_x(add_half(straight[:count], crossed[count:]), xi)
        now = back_x(add_half(now[0], to_other_z(now[1])), xi)
        out = [shape(base.shape, BF)]
        return kernel_call(final_kernel, out, [where, base, hot0, hot1] + before + now, smem_first=True)[0]

    fwd_end = finish(base_fwd, own_fwd0, own[1], fwd_straight, fwd_crossed, fwd1)
    cot_end = finish(base_cot, own_cot0, own[3], cot_straight, cot_crossed, cot1)
    return (fwd_end[None], cot_end[None])


def solution(mesh):
    split = Mesh(mesh.devices.reshape(-1, NX, NZ), ("section", "x", "zh"))
    expert = ("x", "zh")
    placed = (
        P("section", expert, None),
        P(None, expert, None),
        P("section", expert, None),
        P(None, expert, None),
        P(None, "section", expert, None),
        P("section", None),
        P("section", None, None, expert),
        P("section", None, None, expert),
        P("section", None, expert, None),
        P(None, "section", None, None),
        P(None, "section", None, None),
        P(None, "section", None, None),
        P(None, "section", None, None),
    )
    return jax.shard_map(
        on_device,
        mesh=split,
        in_specs=placed,
        out_specs=(P("section", expert, None), P("section", expert, None)),
        check_vma=False,
    )
```

```python
import functools

import jax
import jax.numpy as jnp
from jax import lax
from jax.experimental import pallas as pl
from jax.experimental.pallas import tpu as pltpu
from jax.sharding import Mesh, PartitionSpec as P

CAP = 16
NX = 4
NZ = 2
EPSILON = 1e-06
BF = jnp.bfloat16
F32 = jnp.float32


def dot(a, b, contract=(1, 0)):
    dims = (((contract[0],), (contract[1],)), ((), ()))
    return lax.dot_general(a, b, dims, preferred_element_type=F32)


def to_x(block, distance):
    route = [(i, (i + distance) % NX) for i in range(NX)]
    return lax.ppermute(block, "x", route)


def to_other_z(block):
    return lax.ppermute(block, "zh", [(0, 1), (1, 0)])


def to_section(block, step, flip=0):
    count = lax.axis_size("section")
    route = []
    for s in range(count):
        if 0 <= s + step < count:
            for z in range(NZ):
                route.append((s * NZ + z, (s + step) * NZ + (z ^ flip)))
    return lax.ppermute(block, ("section", "zh"), route)


def routing_plans(ids, weights, zi):
    plans = ids.shape[0]
    matches = (ids == 0).astype(F32)
    mixing = jnp.sum(weights * matches, axis=-1).reshape(plans, NX, NZ, -1)
    member = jnp.sum(matches, axis=-1).reshape(plans, NX, NZ, -1)
    rows = member.shape[-1]
    swap = lambda a: jnp.where(zi == 0, a, a[:, :, ::-1])
    mixing = jnp.transpose(swap(mixing), (0, 2, 1, 3))
    member = jnp.transpose(swap(member), (0, 2, 1, 3))
    upto = (lax.broadcasted_iota(jnp.int32, (rows, rows), 0) <= lax.broadcasted_iota(jnp.int32, (rows, rows), 1)).astype(BF)
    order = dot(member.reshape(-1, rows).astype(BF), upto).reshape(member.shape)
    slot = jnp.where(member > 0, order, 0.0)
    wanted = jnp.arange(1, CAP + 1, dtype=jnp.int32).astype(F32)
    one_hot = (slot[..., None, :] == wanted[:, None]).astype(F32)
    spread = jnp.broadcast_to(mixing[..., None, :], one_hot.shape)
    slot_weight = jnp.sum((one_hot * spread).reshape(plans, -1, rows), axis=-1, keepdims=True)
    return one_hot.astype(BF), slot_weight


def after(value, *before):
    return lax.optimization_barrier((value,) + before)[0]


def two_words(column):
    high = lax.reduce_precision(column, 8, 7)
    low = column - high
    lane = lax.broadcasted_iota(jnp.int32, (column.shape[0], 128), 1)
    return jnp.where(lane == 0, high, jnp.where(lane == 1, low, 0.0)).astype(BF)


def kernel_call(kernel, outs, operands, smem_first=False, scratch=()):
    specs = [pl.BlockSpec(memory_space=pltpu.VMEM) for _ in operands]
    if smem_first:
        specs[0] = pl.BlockSpec(memory_space=pltpu.SMEM)
    return pl.pallas_call(
        kernel,
        out_shape=outs,
        in_specs=specs,
        out_specs=[pl.BlockSpec(memory_space=pltpu.VMEM) for _ in outs],
        scratch_shapes=list(scratch),
        cost_estimate=pl.CostEstimate(flops=1000, bytes_accessed=1000, transcendentals=0),
        compiler_params=pltpu.CompilerParams(vmem_limit_bytes=14 * 2**20),
    )(*operands)


def shape(dims, dtype):
    return jax.ShapeDtypeStruct(dims, dtype)


def column_block(index, width):
    return pl.ds(pl.multiple_of(lax.rem(index, NX) * width, 128), width)


def pack_kernel(where, hot, fwd, stash, cot, *rest):
    outs, (hat1, word1, packed) = rest[:NX], rest[NX:]
    width = outs[0].shape[-1]
    x_fwd = dot(hot[0], fwd[...])
    x_bwd = dot(hot[2], stash[0])
    x_next = dot(hot[3], stash[1])
    g = dot(hot[2], cot[...])

    def inverse(x):
        return lax.rsqrt(jnp.mean(x * x, axis=-1, keepdims=True) + EPSILON)

    inv0, inv1 = inverse(x_bwd), inverse(x_next)
    packed[0] = (x_fwd * inverse(x_fwd)).astype(BF)
    packed[1] = (x_bwd * inv0).astype(BF)
    packed[2] = (g * inv0).astype(BF)
    hat1[...] = (x_next * inv1).astype(BF)
    word1[...] = jnp.broadcast_to(inv1, word1.shape)
    for d in range(NX):
        outs[d][...] = packed[:, :, column_block(where[0] + d, width)]


def pack_later_kernel(hot, fwd, cot, word1, out):
    depth = fwd.shape[-1]
    inv1 = word1[:, :1]
    out[0, :, :depth] = dot(hot[1], fwd[...]).astype(BF)
    out[1, :, :depth] = (dot(hot[3], cot[...]) * inv1).astype(BF)
    words = two_words(inv1)
    for i in range(2):
        out[i, :, depth:] = words


def weights_kernel(where, gate, up, down, *outs):
    width, half = gate.shape[0] // NX, gate.shape[1]
    for d in range(NX):
        at = pl.multiple_of(lax.rem(where[0] + d, NX) * width, 128)
        outs[d][:width, :half] = gate[pl.ds(at, width), :]
        outs[d][:width, half:] = up[pl.ds(at, width), :]
        for j in range(width // (2 * half)):
            to = width + j * half
            outs[d][to : to + half, :] = down[:, pl.ds(at + j * 2 * half, 2 * half)]


def down_blocks(weights):
    wide = weights.shape[1]
    half = wide // 2
    blocks = weights.shape[0] // (wide + half)
    for j in range(blocks):
        to = blocks * wide + j * half
        yield slice(j * wide, (j + 1) * wide), slice(to, to + half)


def times_down(hidden, weights, outs):
    for columns, lines in down_blocks(weights[0]):
        value = sum(dot(h, w[lines, :]) for h, w in zip(hidden, weights))
        put(outs, value, columns)


def times_down_back(x, weights):
    return sum(dot(x[:, columns], weights[lines, :], (1, 1)) for columns, lines in down_blocks(weights))


def split_kernel(where, own, other, own_hat, other_hat, *outs):
    width = own_hat.shape[-1] // NX
    for d in range(NX):
        at = column_block(where[0] + d, width)
        for side, (rows, hat) in enumerate(((own, own_hat), (other, other_hat))):
            lines = slice(side * CAP, (side + 1) * CAP)
            outs[d][:2, lines, :width] = rows[:, :, at]
            outs[d][:2, lines, width:] = rows[:, :, NX * width :]
            outs[d][2, lines, :width] = hat[:, at]
            outs[d][2, lines, width:] = rows[1, :, NX * width :]


def order_kernel(where, *refs):
    pieces, outs = refs[:NX], refs[NX:]
    for d in range(NX):
        at = pl.multiple_of(lax.rem(where[0] + NX - d, NX) * CAP, CAP)
        for side, out in enumerate(outs):
            out[:, pl.ds(at, CAP), :] = pieces[d][:, side * CAP : (side + 1) * CAP, :]


def both(own, other, index, width):
    return jnp.concatenate([own[index, :, :width], other[index, :, :width]], axis=0)


def gained(x, gain):
    return (x.astype(F32) * gain[...]).astype(BF)


def first_kernel(own, other, gain, *refs):
    weights, outs = refs[:NX], refs[NX:]
    width = gain.shape[-1]
    x_fwd = gained(both(own, other, 0, width), gain)
    x_bwd = gained(both(own, other, 1, width), gain)
    cot = both(own, other, 2, width)
    rows = x_fwd.shape[0]
    for w, out in zip(weights, outs):
        out[:rows, :] = dot(x_fwd, w[:width, :]).astype(out.dtype)
        out[rows : 2 * rows, :] = dot(x_bwd, w[:width, :]).astype(out.dtype)
        hidden_cot = times_down_back(cot, w).astype(out.dtype)
        out[2 * rows :, : w.shape[1] // 2] = hidden_cot[: rows // 2]
        out[2 * rows :, w.shape[1] // 2 :] = hidden_cot[rows // 2 :]


def pre_kernel(index, own, other, gain, *refs):
    weights, outs = refs[:NX], refs[NX:]
    width = gain.shape[-1]
    x = gained(both(own, other, index, width), gain)
    for w, out in zip(weights, outs):
        out[...] = dot(x, w[:width, :]).astype(out.dtype)


def pre_next_kernel(own, other, gain, carry, straight, crossed, *refs):
    weights, outs = refs[:NX], refs[NX:]
    width, wide = gain.shape[-1], weights[0].shape[-1]
    count = straight.shape[0]
    x = both(own, other, 0, width).astype(F32)
    x = x + dot(carry[:, :count], straight[...]) + dot(carry[:, count:], crossed[...])
    squares = two_words(jnp.sum(x * x, axis=-1, keepdims=True))
    x = (x * gain[...]).astype(BF)
    for w, out in zip(weights, outs):
        out[:, :wide] = dot(x, w[:width, :]).astype(out.dtype)
        out[:, wide:] = squares.astype(out.dtype)


def cot_next_kernel(own, other, carry, straight, crossed, *refs):
    weights, outs = refs[:NX], refs[NX:]
    width, count = straight.shape[-1], straight.shape[0]
    words = jnp.concatenate([own[1, :, width:], other[1, :, width:]], axis=0).astype(F32)
    inverse = words[:, :1] + words[:, 1:2]
    moved = dot(carry[:, :count], straight[...]) + dot(carry[:, count:], crossed[...])
    x = (both(own, other, 1, width).astype(F32) + inverse * moved).astype(BF)
    for w, out in zip(weights, outs):
        out[...] = times_down_back(x, w).astype(out.dtype)


def total(parts, rows=slice(None), columns=slice(None)):
    return sum(p[rows, columns].astype(F32) for p in parts)


def hidden_of(gate, up, mix):
    return (gate * jax.nn.sigmoid(gate) * up * mix).astype(BF)


def pair_of(hidden_cot, gate, up):
    sigma = jax.nn.sigmoid(gate)
    gate_cot = hidden_cot * up * sigma * (1.0 + gate * (1.0 - sigma))
    up_cot = hidden_cot * gate * sigma
    along = gate_cot * gate + up_cot * up
    return jnp.concatenate([gate_cot, up_cot, along], axis=1).astype(BF)


def middle_kernel(mix, *refs):
    parts, out = refs[:NX], refs[NX]
    count, half = out.shape[0], parts[0].shape[1] // 2
    pre = total(parts)
    hidden_cot = pre[2 * count :]
    hidden_cot = jnp.concatenate([hidden_cot[:, :half], hidden_cot[:, half:]], axis=0)
    out[:, :half] = hidden_of(pre[:count, :half], pre[:count, half:], mix[0])
    out[:, half:] = pair_of(
        hidden_cot * mix[2], pre[count : 2 * count, :half], pre[count : 2 * count, half:]
    )


def hidden_kernel(depth, mix, *refs):
    parts, out = refs[:NX], refs[NX]
    half = out.shape[1]
    pre = total(parts)
    words = pre[:, 2 * half :]
    scale = lax.rsqrt((words[:, :1] + words[:, 1:2]) / depth + EPSILON)
    out[...] = hidden_of(pre[:, :half] * scale, pre[:, half : 2 * half] * scale, mix[1])


def pair_kernel(mix, *refs):
    cots, parts, out = refs[:NX], refs[NX : 2 * NX], refs[2 * NX]
    half = cots[0].shape[1]
    pre = total(parts)
    out[...] = pair_of(total(cots) * mix[3], pre[:, :half], pre[:, half:])


def put(outs, value, columns=slice(None)):
    at = 0
    for out in outs:
        out[:, columns] = value[at : at + out.shape[0]].astype(out.dtype)
        at += out.shape[0]


def cot_value(pairs, weights, gain, hat):
    width, wide = gain.shape[-1], weights[0].shape[-1]
    normed_cot = sum(dot(p[:, :wide], w[:width, :], (1, 1)) for p, w in zip(pairs, weights))
    along = sum(p[:, wide:].astype(F32) for p in pairs)
    along = jnp.sum(along, axis=-1, keepdims=True) / (NX * width)
    return normed_cot * gain[...] - hat.astype(F32) * along


def ends_kernel(own, other, gain, *refs):
    both_streams, weights, (out_fwd, out_cot) = refs[:NX], refs[NX : 2 * NX], refs[2 * NX :]
    half, width = weights[0].shape[-1] // 2, gain.shape[-1]
    times_down([p[:, :half] for p in both_streams], weights, [out_fwd])
    pairs = [p[:, half:] for p in both_streams]
    put([out_cot], cot_value(pairs, weights, gain, both(own, other, 1, width)))


def ffn_kernel(*refs):
    hidden, weights, outs = refs[:NX], refs[NX : 2 * NX], refs[2 * NX :]
    times_down([h[...] for h in hidden], weights, outs)


def cot_out_kernel(own, other, gain, *refs):
    pairs, weights, outs = refs[:NX], refs[NX : 2 * NX], refs[2 * NX :]
    pairs = [p[...] for p in pairs]
    put(outs, cot_value(pairs, weights, gain, both(own, other, 2, gain.shape[-1])))


def final_kernel(where, base, hot0, hot1, *refs):
    before, now, out = refs[:NX], refs[NX : 2 * NX], refs[2 * NX]
    width = before[0].shape[-1]
    for d in range(NX):
        at = column_block(where[0] + NX - d, width)
        rows = base[:, at].astype(F32) + dot(hot0[...], before[d][...])
        rows = rows.astype(BF).astype(F32) + dot(hot1[...], now[d][...], (0, 0))
        out[:, at] = rows.astype(BF)


def back_x(delta, xi):
    pieces = []
    for d in range(NX):
        part = lax.dynamic_slice_in_dim(delta, ((xi + d) % NX) * CAP, CAP, 0)
        pieces.append(part if d == 0 else to_x(part, d))
    return pieces


def gather_x(block):
    return [block] + [to_x(block, d) for d in range(1, NX)]


def sum_parts(parts):
    return [parts[0]] + [to_x(parts[d], -d) for d in range(1, NX)]


def on_device(
    forward_in,
    entering,
    cotangent_in,
    cot_entering,
    stash,
    norm_gain,
    w_gate,
    w_up,
    w_down,
    ids_fwd,
    route_fwd,
    ids_bwd,
    route_bwd,
):
    section = lax.axis_index("section")
    last = lax.axis_size("section") - 1
    xi = lax.axis_index("x")
    zi = lax.axis_index("zh")
    depth = stash.shape[-1]
    width = depth // NX
    half = w_gate.shape[-1]
    rows = NZ * NX * CAP

    ids = jnp.concatenate([ids_fwd[:, 0], ids_bwd[:, 0]], axis=0)
    routes = jnp.concatenate([route_fwd[:, 0], route_bwd[:, 0]], axis=0)
    hot, mix = routing_plans(ids, routes, zi)
    own = lax.dynamic_index_in_dim(hot[:, 0], xi, 1, keepdims=False)
    flat = hot.reshape(4, rows, -1)

    where = xi.astype(jnp.int32).reshape(1)

    wide = [shape((3, CAP, width), BF)] * NX
    *first, hat1, word1 = kernel_call(
        pack_kernel,
        wide + [shape((CAP, depth), BF), shape((CAP, 128), F32)],
        [where, own, forward_in[0], stash[:, 0], cotangent_in[0]],
        smem_first=True,
        scratch=[pltpu.VMEM((3, CAP, depth), BF)],
    )
    first = [first[0]] + [to_x(first[d], d) for d in range(1, NX)]

    weights = kernel_call(
        weights_kernel,
        [shape((width + width // 2, 2 * half), BF)] * NX,
        [where, after(w_gate[0, 0], hat1), w_up[0, 0], w_down[0, 0]],
        smem_first=True,
    )
    weights = [weights[0]] + [to_x(weights[d], d) for d in range(1, NX)]
    gain = lax.dynamic_slice_in_dim(norm_gain, xi * width, width, 1)

    def in_order(pieces, sides):
        count, _, columns = pieces[0].shape
        outs = [shape((count, NX * CAP, columns), BF)] * sides
        return kernel_call(order_kernel, outs, [where] + pieces, smem_first=True)

    first_own = in_order(first, 1)[0]
    first_other = to_other_z(first_own)

    turned = jnp.swapaxes(flat, 1, 2)
    moved_fwd = to_section(jnp.concatenate([forward_in[0], turned[0]], axis=1), 1)
    moved_cot = to_section(jnp.concatenate([cotangent_in[0], turned[2]], axis=1), -1)
    base_fwd = jnp.where(section == 0, entering[0], moved_fwd[:, :depth])
    base_cot = jnp.where(section == last, cot_entering[0], moved_cot[:, :depth])
    hot_fwd, hot_cot = moved_fwd[:, depth:], moved_cot[:, depth:]
    later = kernel_call(
        pack_later_kernel,
        [shape((2, CAP, depth + 128), BF)],
        [own, base_fwd, base_cot, word1],
    )[0]
    later_far = to_other_z(after(later, first_other))
    hat1_far = to_other_z(after(hat1, later_far))

    def cross_x(*before):
        pieces = kernel_call(
            split_kernel,
            [shape((3, 2 * CAP, width + 128), BF)] * NX,
            [where, after(later, *before), later_far, hat1, hat1_far],
            smem_first=True,
        )
        return in_order([pieces[0]] + [to_x(pieces[d], d) for d in range(1, NX)], 2)

    group = jnp.arange(rows) // CAP
    same = (group[:, None] == group[None, :]).astype(F32)

    def carry(plan, before):
        move = (dot(flat[plan], before) * same).astype(BF)
        return jnp.concatenate([move, jnp.roll(move, NX * CAP, axis=1)], axis=1)

    carry_fwd = carry(1, hot_fwd)
    carry_cot = carry(3, hot_cot)
    own_fwd0 = lax.dynamic_slice_in_dim(hot_fwd, xi * CAP, CAP, 1)
    own_cot0 = lax.dynamic_slice_in_dim(hot_cot, xi * CAP, CAP, 1)

    def parts_of(kernel, operands, columns, count):
        outs = [shape((count, columns), F32)] + [shape((count, columns), BF)] * (NX - 1)
        return kernel_call(kernel, outs, operands)

    whole = [shape((rows, width), BF)]
    halves = [shape((NX * CAP, width), BF)] * 2

    parts = sum_parts(
        parts_of(
            first_kernel,
            [after(first_own, later_far), first_other, gain] + weights,
            2 * half,
            2 * rows + rows // 2,
        )
    )
    middle = [shape((rows, 4 * half), BF)]
    middle = kernel_call(middle_kernel, middle, [after(mix, hat1_far)] + parts)[0]
    fwd0, cot0 = kernel_call(
        ends_kernel, whole * 2, [first_own, first_other, gain] + gather_x(middle) + weights
    )
    fwd_crossed = to_section(fwd0, 1, 1)
    fwd_straight = to_section(fwd0, 1)
    cot_crossed = to_section(cot0, -1, 1)
    cot_straight = to_section(cot0, -1)

    later_own, later_other = cross_x(fwd_crossed, fwd_straight, cot_straight)
    next_pre = sum_parts(
        parts_of(
            pre_next_kernel,
            [later_own, later_other, gain, carry_fwd, fwd_straight, fwd_crossed] + weights,
            3 * half,
            rows,
        )
    )
    hidden_kind = [shape((rows, half), BF)]
    hidden1 = kernel_call(functools.partial(hidden_kernel, depth), hidden_kind, [mix] + next_pre)[0]
    pre1 = sum_parts(
        parts_of(
            functools.partial(pre_kernel, 2), [later_own, later_other, gain] + weights, 2 * half, rows
        )
    )
    cots1 = sum_parts(
        parts_of(
            cot_next_kernel,
            [later_own, later_other, carry_cot, after(cot_straight, hidden1), cot_crossed] + weights,
            half,
            rows,
        )
    )
    fwd1 = kernel_call(ffn_kernel, halves, gather_x(hidden1) + weights)
    cots1 = [after(cots1[0], fwd1[0])] + cots1[1:]
    pair1 = kernel_call(pair_kernel, [shape((rows, 3 * half), BF)], [mix] + cots1 + pre1)[0]
    cot1 = kernel_call(
        cot_out_kernel, halves, [later_own, later_other, gain] + gather_x(pair1) + weights
    )

    def add_half(a, b):
        return (a.astype(F32) + b.astype(F32)).astype(BF)

    def finish(base, hot0, hot1, straight, crossed, now):
        count = NX * CAP
        before = back_x(add_half(straight[:count], crossed[count:]), xi)
        now = back_x(add_half(now[0], to_other_z(now[1])), xi)
        out = [shape(base.shape, BF)]
        return kernel_call(final_kernel, out, [where, base, hot0, hot1] + before + now, smem_first=True)[0]

    fwd_end = finish(base_fwd, own_fwd0, own[1], fwd_straight, fwd_crossed, fwd1)
    cot_end = finish(base_cot, own_cot0, own[3], cot_straight, cot_crossed, cot1)
    return (fwd_end[None], cot_end[None])


def solution(mesh):
    split = Mesh(mesh.devices.reshape(-1, NX, NZ), ("section", "x", "zh"))
    expert = ("x", "zh")
    placed = (
        P("section", expert, None),
        P(None, expert, None),
        P("section", expert, None),
        P(None, expert, None),
        P(None, "section", expert, None),
        P("section", None),
        P("section", None, None, expert),
        P("section", None, None, expert),
        P("section", None, expert, None),
        P(None, "section", None, None),
        P(None, "section", None, None),
        P(None, "section", None, None),
        P(None, "section", None, None),
    )
    return jax.shard_map(
        on_device,
        mesh=split,
        in_specs=placed,
        out_specs=(P("section", expert, None), P("section", expert, None)),
        check_vma=False,
    )
```

```python
import functools

import jax
import jax.numpy as jnp
from jax import lax
from jax.experimental import pallas as pl
from jax.experimental.pallas import tpu as pltpu
from jax.sharding import Mesh, PartitionSpec as P

CAP = 16
NX = 4
NZ = 2
EPSILON = 1e-06
BF = jnp.bfloat16
F32 = jnp.float32


def dot(a, b, contract=(1, 0)):
    dims = (((contract[0],), (contract[1],)), ((), ()))
    return lax.dot_general(a, b, dims, preferred_element_type=F32)


def to_x(block, distance):
    route = [(i, (i + distance) % NX) for i in range(NX)]
    return lax.ppermute(block, "x", route)


def to_other_z(block):
    return lax.ppermute(block, "zh", [(0, 1), (1, 0)])


def to_section(block, step, flip=0):
    count = lax.axis_size("section")
    route = []
    for s in range(count):
        if 0 <= s + step < count:
            for z in range(NZ):
                route.append((s * NZ + z, (s + step) * NZ + (z ^ flip)))
    return lax.ppermute(block, ("section", "zh"), route)


def routing_plans(ids, weights, zi):
    plans = ids.shape[0]
    matches = (ids == 0).astype(F32)
    mixing = jnp.sum(weights * matches, axis=-1).reshape(plans, NX, NZ, -1)
    member = jnp.sum(matches, axis=-1).reshape(plans, NX, NZ, -1)
    rows = member.shape[-1]
    swap = lambda a: jnp.where(zi == 0, a, a[:, :, ::-1])
    mixing = jnp.transpose(swap(mixing), (0, 2, 1, 3))
    member = jnp.transpose(swap(member), (0, 2, 1, 3))
    upto = (lax.broadcasted_iota(jnp.int32, (rows, rows), 0) <= lax.broadcasted_iota(jnp.int32, (rows, rows), 1)).astype(BF)
    order = dot(member.reshape(-1, rows).astype(BF), upto).reshape(member.shape)
    slot = jnp.where(member > 0, order, 0.0)
    wanted = jnp.arange(1, CAP + 1, dtype=jnp.int32).astype(F32)
    one_hot = (slot[..., None, :] == wanted[:, None]).astype(F32)
    spread = jnp.broadcast_to(mixing[..., None, :], one_hot.shape)
    slot_weight = jnp.sum((one_hot * spread).reshape(plans, -1, rows), axis=-1, keepdims=True)
    return one_hot.astype(BF), slot_weight


def after(value, *before):
    return lax.optimization_barrier((value,) + before)[0]


def two_words(column):
    high = lax.reduce_precision(column, 8, 7)
    low = column - high
    lane = lax.broadcasted_iota(jnp.int32, (column.shape[0], 128), 1)
    return jnp.where(lane == 0, high, jnp.where(lane == 1, low, 0.0)).astype(BF)


def kernel_call(kernel, outs, operands, smem_first=False, scratch=(), room=14):
    specs = [pl.BlockSpec(memory_space=pltpu.VMEM) for _ in operands]
    if smem_first:
        specs[0] = pl.BlockSpec(memory_space=pltpu.SMEM)
    return pl.pallas_call(
        kernel,
        out_shape=outs,
        in_specs=specs,
        out_specs=[pl.BlockSpec(memory_space=pltpu.VMEM) for _ in outs],
        scratch_shapes=list(scratch),
        cost_estimate=pl.CostEstimate(flops=1000, bytes_accessed=1000, transcendentals=0),
        compiler_params=pltpu.CompilerParams(vmem_limit_bytes=room * 2**20),
    )(*operands)


def shape(dims, dtype):
    return jax.ShapeDtypeStruct(dims, dtype)


def column_block(index, width):
    return pl.ds(pl.multiple_of(lax.rem(index, NX) * width, 128), width)


def pack_kernel(where, hot, fwd, stash, cot, *rest):
    outs, (hat1, word1, packed) = rest[:NX], rest[NX:]
    width = outs[0].shape[-1]
    x_fwd = dot(hot[0], fwd[...])
    x_bwd = dot(hot[2], stash[0])
    x_next = dot(hot[3], stash[1])
    g = dot(hot[2], cot[...])

    def inverse(x):
        return lax.rsqrt(jnp.mean(x * x, axis=-1, keepdims=True) + EPSILON)

    inv0, inv1 = inverse(x_bwd), inverse(x_next)
    packed[0] = (x_fwd * inverse(x_fwd)).astype(BF)
    packed[1] = (x_bwd * inv0).astype(BF)
    packed[2] = (g * inv0).astype(BF)
    hat1[...] = (x_next * inv1).astype(BF)
    word1[...] = jnp.broadcast_to(inv1, word1.shape)
    for d in range(NX):
        outs[d][...] = packed[:, :, column_block(where[0] + d, width)]


def pack_later_kernel(hot, fwd, cot, word1, out):
    depth = fwd.shape[-1]
    inv1 = word1[:, :1]
    out[0, :, :depth] = dot(hot[1], fwd[...]).astype(BF)
    out[1, :, :depth] = (dot(hot[3], cot[...]) * inv1).astype(BF)
    words = two_words(inv1)
    for i in range(2):
        out[i, :, depth:] = words


def weights_kernel(where, gate, up, down, *outs):
    width, half = gate.shape[0] // NX, gate.shape[1]
    for d in range(NX):
        at = pl.multiple_of(lax.rem(where[0] + d, NX) * width, 128)
        outs[d][:width, :half] = gate[pl.ds(at, width), :]
        outs[d][:width, half:] = up[pl.ds(at, width), :]
        for j in range(width // (2 * half)):
            to = width + j * half
            outs[d][to : to + half, :] = down[:, pl.ds(at + j * 2 * half, 2 * half)]


def down_blocks(weights):
    wide = weights.shape[1]
    half = wide // 2
    blocks = weights.shape[0] // (wide + half)
    for j in range(blocks):
        to = blocks * wide + j * half
        yield slice(j * wide, (j + 1) * wide), slice(to, to + half)


def times_down(hidden, weights, outs):
    for columns, lines in down_blocks(weights[0]):
        value = sum(dot(h, w[lines, :]) for h, w in zip(hidden, weights))
        put(outs, value, columns)


def times_down_back(x, weights):
    return sum(dot(x[:, columns], weights[lines, :], (1, 1)) for columns, lines in down_blocks(weights))


def split_kernel(where, own, other, own_hat, other_hat, *outs):
    width = own_hat.shape[-1] // NX
    for d in range(NX):
        at = column_block(where[0] + d, width)
        for side, (rows, hat) in enumerate(((own, own_hat), (other, other_hat))):
            lines = slice(side * CAP, (side + 1) * CAP)
            outs[d][:2, lines, :width] = rows[:, :, at]
            outs[d][:2, lines, width:] = rows[:, :, NX * width :]
            outs[d][2, lines, :width] = hat[:, at]
            outs[d][2, lines, width:] = rows[1, :, NX * width :]


def order_kernel(where, *refs):
    pieces, outs = refs[:NX], refs[NX:]
    for d in range(NX):
        at = pl.multiple_of(lax.rem(where[0] + NX - d, NX) * CAP, CAP)
        for side, out in enumerate(outs):
            out[:, pl.ds(at, CAP), :] = pieces[d][:, side * CAP : (side + 1) * CAP, :]


def both(own, other, index, width):
    return jnp.concatenate([own[index, :, :width], other[index, :, :width]], axis=0)


def gained(x, gain):
    return (x.astype(F32) * gain[...]).astype(BF)


def first_kernel(own, other, gain, *refs):
    weights, outs = refs[:NX], refs[NX:]
    width = gain.shape[-1]
    x_fwd = gained(both(own, other, 0, width), gain)
    x_bwd = gained(both(own, other, 1, width), gain)
    cot = both(own, other, 2, width)
    rows = x_fwd.shape[0]
    for w, out in zip(weights, outs):
        out[:rows, :] = dot(x_fwd, w[:width, :]).astype(out.dtype)
        out[rows : 2 * rows, :] = dot(x_bwd, w[:width, :]).astype(out.dtype)
        hidden_cot = times_down_back(cot, w).astype(out.dtype)
        out[2 * rows :, : w.shape[1] // 2] = hidden_cot[: rows // 2]
        out[2 * rows :, w.shape[1] // 2 :] = hidden_cot[rows // 2 :]


def pre_next_kernel(own, other, gain, carry, straight, crossed, *refs):
    weights, outs = refs[:NX], refs[NX:]
    width, wide = gain.shape[-1], weights[0].shape[-1]
    count = straight.shape[0]
    x = both(own, other, 0, width).astype(F32)
    x = x + dot(carry[:, :count], straight[...]) + dot(carry[:, count:], crossed[...])
    squares = two_words(jnp.sum(x * x, axis=-1, keepdims=True))
    x = (x * gain[...]).astype(BF)
    for w, out in zip(weights, outs):
        out[:, :wide] = dot(x, w[:width, :]).astype(out.dtype)
        out[:, wide:] = squares.astype(out.dtype)


def cot_next_kernel(own, other, gain, carry, straight, crossed, *refs):
    weights, outs = refs[:NX], refs[NX:]
    width, count = straight.shape[-1], straight.shape[0]
    words = jnp.concatenate([own[1, :, width:], other[1, :, width:]], axis=0).astype(F32)
    inverse = words[:, :1] + words[:, 1:2]
    moved = dot(carry[:, :count], straight[...]) + dot(carry[:, count:], crossed[...])
    x = (both(own, other, 1, width).astype(F32) + inverse * moved).astype(BF)
    hat = gained(both(own, other, 2, width), gain)
    wide = weights[0].shape[-1]
    for w, out in zip(weights, outs):
        out[:, :wide] = dot(hat, w[:width, :]).astype(out.dtype)
        out[:, wide:] = times_down_back(x, w).astype(out.dtype)


def total(parts, rows=slice(None), columns=slice(None)):
    return sum(p[rows, columns].astype(F32) for p in parts)


def hidden_of(gate, up, mix):
    return (gate * jax.nn.sigmoid(gate) * up * mix).astype(BF)


def pair_of(hidden_cot, gate, up):
    sigma = jax.nn.sigmoid(gate)
    gate_cot = hidden_cot * up * sigma * (1.0 + gate * (1.0 - sigma))
    up_cot = hidden_cot * gate * sigma
    along = gate_cot * gate + up_cot * up
    return jnp.concatenate([gate_cot, up_cot, along], axis=1).astype(BF)


def middle_kernel(mix, *refs):
    parts, out = refs[:NX], refs[NX]
    count, half = out.shape[0], parts[0].shape[1] // 2
    pre = total(parts)
    hidden_cot = pre[2 * count :]
    hidden_cot = jnp.concatenate([hidden_cot[:, :half], hidden_cot[:, half:]], axis=0)
    out[:, :half] = hidden_of(pre[:count, :half], pre[:count, half:], mix[0])
    out[:, half:] = pair_of(
        hidden_cot * mix[2], pre[count : 2 * count, :half], pre[count : 2 * count, half:]
    )


def hidden_kernel(depth, mix, *refs):
    parts, out = refs[:NX], refs[NX]
    half = out.shape[1]
    pre = total(parts)
    words = pre[:, 2 * half :]
    scale = lax.rsqrt((words[:, :1] + words[:, 1:2]) / depth + EPSILON)
    out[...] = hidden_of(pre[:, :half] * scale, pre[:, half : 2 * half] * scale, mix[1])


def pair_kernel(mix, *refs):
    parts, out = refs[:NX], refs[NX]
    half = out.shape[1] // 3
    pre = total(parts)
    out[...] = pair_of(pre[:, 2 * half :] * mix[3], pre[:, :half], pre[:, half : 2 * half])


def put(outs, value, columns=slice(None)):
    at = 0
    for out in outs:
        out[:, columns] = value[at : at + out.shape[0]].astype(out.dtype)
        at += out.shape[0]


def cot_value(pairs, weights, gain, hat):
    width, wide = gain.shape[-1], weights[0].shape[-1]
    normed_cot = sum(dot(p[:, :wide], w[:width, :], (1, 1)) for p, w in zip(pairs, weights))
    along = sum(p[:, wide:].astype(F32) for p in pairs)
    along = jnp.sum(along, axis=-1, keepdims=True) / (NX * width)
    return normed_cot * gain[...] - hat.astype(F32) * along


def ends_kernel(own, other, gain, *refs):
    both_streams, weights, (out_fwd, out_cot) = refs[:NX], refs[NX : 2 * NX], refs[2 * NX :]
    half, width = weights[0].shape[-1] // 2, gain.shape[-1]
    times_down([p[:, :half] for p in both_streams], weights, [out_fwd])
    pairs = [p[:, half:] for p in both_streams]
    put([out_cot], cot_value(pairs, weights, gain, both(own, other, 1, width)))


def ffn_kernel(*refs):
    hidden, weights, outs = refs[:NX], refs[NX : 2 * NX], refs[2 * NX :]
    times_down([h[...] for h in hidden], weights, outs)


def cot_out_kernel(own, other, gain, *refs):
    pairs, weights, outs = refs[:NX], refs[NX : 2 * NX], refs[2 * NX :]
    pairs = [p[...] for p in pairs]
    put(outs, cot_value(pairs, weights, gain, both(own, other, 2, gain.shape[-1])))


def final_kernel(where, base, hot0, hot1, *refs):
    before, now, out = refs[:NX], refs[NX : 2 * NX], refs[2 * NX]
    width = before[0].shape[-1]
    for d in range(NX):
        at = column_block(where[0] + NX - d, width)
        rows = base[:, at].astype(F32) + dot(hot0[...], before[d][...])
        rows = rows.astype(BF).astype(F32) + dot(hot1[...], now[d][...], (0, 0))
        out[:, at] = rows.astype(BF)


def back_x(delta, xi):
    pieces = []
    for d in range(NX):
        part = lax.dynamic_slice_in_dim(delta, ((xi + d) % NX) * CAP, CAP, 0)
        pieces.append(part if d == 0 else to_x(part, d))
    return pieces


def gather_x(block):
    return [block] + [to_x(block, d) for d in range(1, NX)]


def sum_parts(parts):
    return [parts[0]] + [to_x(parts[d], -d) for d in range(1, NX)]


def on_device(
    forward_in,
    entering,
    cotangent_in,
    cot_entering,
    stash,
    norm_gain,
    w_gate,
    w_up,
    w_down,
    ids_fwd,
    route_fwd,
    ids_bwd,
    route_bwd,
):
    section = lax.axis_index("section")
    last = lax.axis_size("section") - 1
    xi = lax.axis_index("x")
    zi = lax.axis_index("zh")
    depth = stash.shape[-1]
    width = depth // NX
    half = w_gate.shape[-1]
    rows = NZ * NX * CAP

    ids = jnp.concatenate([ids_fwd[:, 0], ids_bwd[:, 0]], axis=0)
    routes = jnp.concatenate([route_fwd[:, 0], route_bwd[:, 0]], axis=0)
    hot, mix = routing_plans(ids, routes, zi)
    own = lax.dynamic_index_in_dim(hot[:, 0], xi, 1, keepdims=False)
    flat = hot.reshape(4, rows, -1)

    where = xi.astype(jnp.int32).reshape(1)

    wide = [shape((3, CAP, width), BF)] * NX
    *first, hat1, word1 = kernel_call(
        pack_kernel,
        wide + [shape((CAP, depth), BF), shape((CAP, 128), F32)],
        [where, own, forward_in[0], stash[:, 0], cotangent_in[0]],
        smem_first=True,
        scratch=[pltpu.VMEM((3, CAP, depth), BF)],
        room=44,
    )
    first = [first[0]] + [to_x(first[d], d) for d in range(1, NX)]

    def in_order(pieces, sides, room=14):
        count, _, columns = pieces[0].shape
        outs = [shape((count, NX * CAP, columns), BF)] * sides
        return kernel_call(order_kernel, outs, [where] + pieces, smem_first=True, room=room)

    first_own = in_order(first, 1, 44)[0]
    first_other = to_other_z(first_own)

    weights = kernel_call(
        weights_kernel,
        [shape((width + width // 2, 2 * half), BF)] * NX,
        [where, after(w_gate[0, 0], first_own), w_up[0, 0], w_down[0, 0]],
        smem_first=True,
        room=44,
    )
    weights = [weights[0]] + [to_x(weights[d], d) for d in range(1, NX)]
    gain = lax.dynamic_slice_in_dim(norm_gain, xi * width, width, 1)

    turned = jnp.swapaxes(flat, 1, 2)
    turned = after(turned, weights[0])
    moved_fwd = to_section(jnp.concatenate([forward_in[0], turned[0]], axis=1), 1)
    moved_cot = to_section(jnp.concatenate([cotangent_in[0], turned[2]], axis=1), -1)
    base_fwd = jnp.where(section == 0, entering[0], moved_fwd[:, :depth])
    base_cot = jnp.where(section == last, cot_entering[0], moved_cot[:, :depth])
    hot_fwd, hot_cot = moved_fwd[:, depth:], moved_cot[:, depth:]
    later = kernel_call(
        pack_later_kernel,
        [shape((2, CAP, depth + 128), BF)],
        [own, base_fwd, base_cot, word1],
    )[0]
    later_far = to_other_z(after(later, first_other))

    def cross_x(hat1_far, *before):
        pieces = kernel_call(
            split_kernel,
            [shape((3, 2 * CAP, width + 128), BF)] * NX,
            [where, after(later, *before), later_far, hat1, hat1_far],
            smem_first=True,
        )
        return in_order([pieces[0]] + [to_x(pieces[d], d) for d in range(1, NX)], 2)

    group = jnp.arange(rows) // CAP
    same = (group[:, None] == group[None, :]).astype(F32)

    def carry(plan, before):
        move = (dot(flat[plan], before) * same).astype(BF)
        return jnp.concatenate([move, jnp.roll(move, NX * CAP, axis=1)], axis=1)

    carry_fwd = carry(1, hot_fwd)
    carry_cot = carry(3, hot_cot)
    own_fwd0 = lax.dynamic_slice_in_dim(hot_fwd, xi * CAP, CAP, 1)
    own_cot0 = lax.dynamic_slice_in_dim(hot_cot, xi * CAP, CAP, 1)

    def parts_of(kernel, operands, columns, count):
        outs = [shape((count, columns), F32)] + [shape((count, columns), BF)] * (NX - 1)
        return kernel_call(kernel, outs, operands)

    whole = [shape((rows, width), BF)]
    halves = [shape((NX * CAP, width), BF)] * 2

    parts = sum_parts(
        parts_of(
            first_kernel,
            [after(first_own, later_far), first_other, gain] + weights,
            2 * half,
            2 * rows + rows // 2,
        )
    )
    hat1_far = to_other_z(after(hat1, parts[0]))
    middle = [shape((rows, 4 * half), BF)]
    middle = kernel_call(middle_kernel, middle, [mix] + parts)[0]
    fwd0, cot0 = kernel_call(
        ends_kernel, whole * 2, [after(first_own, hat1_far), first_other, gain] + gather_x(middle) + weights
    )
    cot_crossed = to_section(cot0, -1, 1)
    cot_straight = to_section(cot0, -1)
    fwd_crossed = to_section(after(fwd0, cot_straight), 1, 1)
    fwd_straight = to_section(fwd0, 1)

    later_own, later_other = cross_x(hat1_far, fwd_straight, cot_straight)
    sums1 = sum_parts(
        parts_of(
            cot_next_kernel,
            [later_own, later_other, gain, carry_cot, cot_straight, cot_crossed] + weights,
            3 * half,
            rows,
        )
    )
    pair1 = kernel_call(pair_kernel, [shape((rows, 3 * half), BF)], [mix] + sums1)[0]
    next_pre = sum_parts(
        parts_of(
            pre_next_kernel,
            [later_own, later_other, gain, after(carry_fwd, pair1), fwd_straight, fwd_crossed]
            + weights,
            3 * half,
            rows,
        )
    )
    cot1 = kernel_call(
        cot_out_kernel, halves, [later_own, later_other, gain] + gather_x(pair1) + weights
    )
    hidden_kind = [shape((rows, half), BF)]
    hidden1 = kernel_call(functools.partial(hidden_kernel, depth), hidden_kind, [mix] + next_pre)[0]
    fwd1 = kernel_call(ffn_kernel, halves, gather_x(hidden1) + weights)

    def add_half(a, b):
        return (a.astype(F32) + b.astype(F32)).astype(BF)

    def finish(base, hot0, hot1, straight, crossed, now):
        count = NX * CAP
        before = back_x(add_half(straight[:count], crossed[count:]), xi)
        now = back_x(add_half(now[0], to_other_z(now[1])), xi)
        out = [shape(base.shape, BF)]
        return kernel_call(final_kernel, out, [where, base, hot0, hot1] + before + now, smem_first=True)[0]

    cot_end = finish(base_cot, own_cot0, own[3], cot_straight, cot_crossed, cot1)
    fwd_end = finish(base_fwd, own_fwd0, own[1], fwd_straight, fwd_crossed, fwd1)
    return (fwd_end[None], cot_end[None])


def solution(mesh):
    split = Mesh(mesh.devices.reshape(-1, NX, NZ), ("section", "x", "zh"))
    expert = ("x", "zh")
    placed = (
        P("section", expert, None),
        P(None, expert, None),
        P("section", expert, None),
        P(None, expert, None),
        P(None, "section", expert, None),
        P("section", None),
        P("section", None, None, expert),
        P("section", None, None, expert),
        P("section", None, expert, None),
        P(None, "section", None, None),
        P(None, "section", None, None),
        P(None, "section", None, None),
        P(None, "section", None, None),
    )
    return jax.shard_map(
        on_device,
        mesh=split,
        in_specs=placed,
        out_specs=(P("section", expert, None), P("section", expert, None)),
        check_vma=False,
    )
```

```python
import functools

import jax
import jax.numpy as jnp
from jax import lax
from jax.experimental import pallas as pl
from jax.experimental.pallas import tpu as pltpu
from jax.sharding import Mesh, PartitionSpec as P

CAP = 16
NX = 4
NZ = 2
EPSILON = 1e-06
BF = jnp.bfloat16
F32 = jnp.float32


def dot(a, b, contract=(1, 0)):
    dims = (((contract[0],), (contract[1],)), ((), ()))
    return lax.dot_general(a, b, dims, preferred_element_type=F32)


def to_x(block, distance):
    route = [(i, (i + distance) % NX) for i in range(NX)]
    return lax.ppermute(block, "x", route)


def to_other_z(block):
    return lax.ppermute(block, "zh", [(0, 1), (1, 0)])


def to_section(block, step, flip=0):
    count = lax.axis_size("section")
    route = []
    for s in range(count):
        if 0 <= s + step < count:
            for z in range(NZ):
                route.append((s * NZ + z, (s + step) * NZ + (z ^ flip)))
    return lax.ppermute(block, ("section", "zh"), route)


def routing_plans(ids, weights, zi):
    plans = ids.shape[0]
    matches = (ids == 0).astype(F32)
    mixing = jnp.sum(weights * matches, axis=-1).reshape(plans, NX, NZ, -1)
    member = jnp.sum(matches, axis=-1).reshape(plans, NX, NZ, -1)
    rows = member.shape[-1]
    swap = lambda a: jnp.where(zi == 0, a, a[:, :, ::-1])
    mixing = jnp.transpose(swap(mixing), (0, 2, 1, 3))
    member = jnp.transpose(swap(member), (0, 2, 1, 3))
    upto = (lax.broadcasted_iota(jnp.int32, (rows, rows), 0) <= lax.broadcasted_iota(jnp.int32, (rows, rows), 1)).astype(BF)
    order = dot(member.reshape(-1, rows).astype(BF), upto).reshape(member.shape)
    slot = jnp.where(member > 0, order, 0.0)
    wanted = jnp.arange(1, CAP + 1, dtype=jnp.int32).astype(F32)
    one_hot = (slot[..., None, :] == wanted[:, None]).astype(F32)
    spread = jnp.broadcast_to(mixing[..., None, :], one_hot.shape)
    slot_weight = jnp.sum((one_hot * spread).reshape(plans, -1, rows), axis=-1, keepdims=True)
    return one_hot.astype(BF), slot_weight


def after(value, *before):
    return lax.optimization_barrier((value,) + before)[0]


def two_words(column):
    high = lax.reduce_precision(column, 8, 7)
    low = column - high
    lane = lax.broadcasted_iota(jnp.int32, (column.shape[0], 128), 1)
    return jnp.where(lane == 0, high, jnp.where(lane == 1, low, 0.0)).astype(BF)


def kernel_call(kernel, outs, operands, smem_first=False, scratch=(), room=14, far=(), far_out=False):
    specs = [
        pl.BlockSpec(memory_space=pl.ANY if i in far else pltpu.VMEM) for i in range(len(operands))
    ]
    if smem_first:
        specs[0] = pl.BlockSpec(memory_space=pltpu.SMEM)
    return pl.pallas_call(
        kernel,
        out_shape=outs,
        in_specs=specs,
        out_specs=[pl.BlockSpec(memory_space=pl.ANY if far_out else pltpu.VMEM) for _ in outs],
        scratch_shapes=list(scratch),
        cost_estimate=pl.CostEstimate(flops=1000, bytes_accessed=1000, transcendentals=0),
        compiler_params=pltpu.CompilerParams(vmem_limit_bytes=room * 2**20),
    )(*operands)


def shape(dims, dtype):
    return jax.ShapeDtypeStruct(dims, dtype)


def column_block(index, width):
    return pl.ds(pl.multiple_of(lax.rem(index, NX) * width, 128), width)


def pack_kernel(where, hot, fwd, stash, cot, *rest):
    outs, (hat1, word1, packed, near_fwd, near_stash, near_cot, sems) = rest[:NX], rest[NX:]
    copies = [
        pltpu.make_async_copy(fwd, near_fwd, sems.at[0]),
        pltpu.make_async_copy(stash, near_stash, sems.at[1]),
        pltpu.make_async_copy(cot, near_cot, sems.at[2]),
    ]
    for copy in copies:
        copy.start()
    for copy in copies:
        copy.wait()
    fwd, stash, cot = near_fwd, near_stash, near_cot
    width = outs[0].shape[-1]
    x_fwd = dot(hot[0], fwd[...])
    x_bwd = dot(hot[2], stash[0])
    x_next = dot(hot[3], stash[1])
    g = dot(hot[2], cot[...])

    def inverse(x):
        return lax.rsqrt(jnp.mean(x * x, axis=-1, keepdims=True) + EPSILON)

    inv0, inv1 = inverse(x_bwd), inverse(x_next)
    packed[0] = (x_fwd * inverse(x_fwd)).astype(BF)
    packed[1] = (x_bwd * inv0).astype(BF)
    packed[2] = (g * inv0).astype(BF)
    hat1[...] = (x_next * inv1).astype(BF)
    word1[...] = jnp.broadcast_to(inv1, word1.shape)
    for d in range(NX):
        outs[d][...] = packed[:, :, column_block(where[0] + d, width)]


def pack_later_kernel(hot, fwd, cot, word1, out):
    depth = fwd.shape[-1]
    inv1 = word1[:, :1]
    out[0, :, :depth] = dot(hot[1], fwd[...]).astype(BF)
    out[1, :, :depth] = (dot(hot[3], cot[...]) * inv1).astype(BF)
    words = two_words(inv1)
    for i in range(2):
        out[i, :, depth:] = words


def weights_kernel(gate, up, down, *refs):
    outs, sems = refs[:NX], refs[NX]
    width, half = gate.shape[0] // NX, gate.shape[1]
    me = lax.axis_index("x")
    copies = []

    def move(source, target):
        copies.append(pltpu.make_async_copy(source, target, sems.at[len(copies)]))
        copies[-1].start()

    for d in (1, 3, 2, 0):
        at = pl.multiple_of(lax.rem(me + d, NX) * width, 128)
        move(gate.at[pl.ds(at, width), :], outs[d].at[:width, :half])
        move(up.at[pl.ds(at, width), :], outs[d].at[:width, half:])
        for j in range(width // (2 * half)):
            to = width + j * half
            across = pl.ds(pl.multiple_of(at + j * 2 * half, 128), 2 * half)
            move(down.at[:, across], outs[d].at[to : to + half, :])
    for copy in copies:
        copy.wait()


def down_blocks(weights):
    wide = weights.shape[1]
    half = wide // 2
    blocks = weights.shape[0] // (wide + half)
    for j in range(blocks):
        to = blocks * wide + j * half
        yield slice(j * wide, (j + 1) * wide), slice(to, to + half)


def times_down(hidden, weights, outs):
    for columns, lines in down_blocks(weights[0]):
        value = sum(dot(h, w[lines, :]) for h, w in zip(hidden, weights))
        put(outs, value, columns)


def times_down_back(x, weights):
    return sum(dot(x[:, columns], weights[lines, :], (1, 1)) for columns, lines in down_blocks(weights))


def split_kernel(where, own, other, own_hat, other_hat, *outs):
    width = own_hat.shape[-1] // NX
    for d in range(NX):
        at = column_block(where[0] + d, width)
        for side, (rows, hat) in enumerate(((own, own_hat), (other, other_hat))):
            lines = slice(side * CAP, (side + 1) * CAP)
            outs[d][:2, lines, :width] = rows[:, :, at]
            outs[d][:2, lines, width:] = rows[:, :, NX * width :]
            outs[d][2, lines, :width] = hat[:, at]
            outs[d][2, lines, width:] = rows[1, :, NX * width :]


def order_kernel(where, *refs):
    pieces, outs = refs[:NX], refs[NX:]
    for d in range(NX):
        at = pl.multiple_of(lax.rem(where[0] + NX - d, NX) * CAP, CAP)
        for side, out in enumerate(outs):
            out[:, pl.ds(at, CAP), :] = pieces[d][:, side * CAP : (side + 1) * CAP, :]


def both(own, other, index, width):
    return jnp.concatenate([own[index, :, :width], other[index, :, :width]], axis=0)


def gained(x, gain):
    return (x.astype(F32) * gain[...]).astype(BF)


def first_kernel(own, other, gain, *refs):
    weights, outs = refs[:NX], refs[NX:]
    width = gain.shape[-1]
    x_fwd = gained(both(own, other, 0, width), gain)
    x_bwd = gained(both(own, other, 1, width), gain)
    cot = both(own, other, 2, width)
    rows = x_fwd.shape[0]
    for w, out in zip(weights, outs):
        out[:rows, :] = dot(x_fwd, w[:width, :]).astype(out.dtype)
        out[rows : 2 * rows, :] = dot(x_bwd, w[:width, :]).astype(out.dtype)
        hidden_cot = times_down_back(cot, w).astype(out.dtype)
        out[2 * rows :, : w.shape[1] // 2] = hidden_cot[: rows // 2]
        out[2 * rows :, w.shape[1] // 2 :] = hidden_cot[rows // 2 :]


def pre_next_kernel(own, other, gain, carry, straight, crossed, *refs):
    weights, outs = refs[:NX], refs[NX:]
    width, wide = gain.shape[-1], weights[0].shape[-1]
    count = straight.shape[0]
    x = both(own, other, 0, width).astype(F32)
    x = x + dot(carry[:, :count], straight[...]) + dot(carry[:, count:], crossed[...])
    squares = two_words(jnp.sum(x * x, axis=-1, keepdims=True))
    x = (x * gain[...]).astype(BF)
    for w, out in zip(weights, outs):
        out[:, :wide] = dot(x, w[:width, :]).astype(out.dtype)
        out[:, wide:] = squares.astype(out.dtype)


def cot_next_kernel(own, other, gain, carry, straight, crossed, *refs):
    weights, outs = refs[:NX], refs[NX:]
    width, count = straight.shape[-1], straight.shape[0]
    words = jnp.concatenate([own[1, :, width:], other[1, :, width:]], axis=0).astype(F32)
    inverse = words[:, :1] + words[:, 1:2]
    moved = dot(carry[:, :count], straight[...]) + dot(carry[:, count:], crossed[...])
    x = (both(own, other, 1, width).astype(F32) + inverse * moved).astype(BF)
    hat = gained(both(own, other, 2, width), gain)
    wide = weights[0].shape[-1]
    for w, out in zip(weights, outs):
        out[:, :wide] = dot(hat, w[:width, :]).astype(out.dtype)
        out[:, wide:] = times_down_back(x, w).astype(out.dtype)


def total(parts, rows=slice(None), columns=slice(None)):
    return sum(p[rows, columns].astype(F32) for p in parts)


def hidden_of(gate, up, mix):
    return (gate * jax.nn.sigmoid(gate) * up * mix).astype(BF)


def pair_of(hidden_cot, gate, up):
    sigma = jax.nn.sigmoid(gate)
    gate_cot = hidden_cot * up * sigma * (1.0 + gate * (1.0 - sigma))
    up_cot = hidden_cot * gate * sigma
    along = gate_cot * gate + up_cot * up
    return jnp.concatenate([gate_cot, up_cot, along], axis=1).astype(BF)


def middle_kernel(mix, *refs):
    parts, out = refs[:NX], refs[NX]
    count, half = out.shape[0], parts[0].shape[1] // 2
    pre = total(parts)
    hidden_cot = pre[2 * count :]
    hidden_cot = jnp.concatenate([hidden_cot[:, :half], hidden_cot[:, half:]], axis=0)
    out[:, :half] = hidden_of(pre[:count, :half], pre[:count, half:], mix[0])
    out[:, half:] = pair_of(
        hidden_cot * mix[2], pre[count : 2 * count, :half], pre[count : 2 * count, half:]
    )


def hidden_kernel(depth, mix, *refs):
    parts, out = refs[:NX], refs[NX]
    half = out.shape[1]
    pre = total(parts)
    words = pre[:, 2 * half :]
    scale = lax.rsqrt((words[:, :1] + words[:, 1:2]) / depth + EPSILON)
    out[...] = hidden_of(pre[:, :half] * scale, pre[:, half : 2 * half] * scale, mix[1])


def pair_kernel(mix, *refs):
    parts, out = refs[:NX], refs[NX]
    half = out.shape[1] // 3
    pre = total(parts)
    out[...] = pair_of(pre[:, 2 * half :] * mix[3], pre[:, :half], pre[:, half : 2 * half])


def put(outs, value, columns=slice(None)):
    at = 0
    for out in outs:
        out[:, columns] = value[at : at + out.shape[0]].astype(out.dtype)
        at += out.shape[0]


def cot_value(pairs, weights, gain, hat):
    width, wide = gain.shape[-1], weights[0].shape[-1]
    normed_cot = sum(dot(p[:, :wide], w[:width, :], (1, 1)) for p, w in zip(pairs, weights))
    along = sum(p[:, wide:].astype(F32) for p in pairs)
    along = jnp.sum(along, axis=-1, keepdims=True) / (NX * width)
    return normed_cot * gain[...] - hat.astype(F32) * along


def ends_kernel(own, other, gain, *refs):
    both_streams, weights, (out_fwd, out_cot) = refs[:NX], refs[NX : 2 * NX], refs[2 * NX :]
    half, width = weights[0].shape[-1] // 2, gain.shape[-1]
    times_down([p[:, :half] for p in both_streams], weights, [out_fwd])
    pairs = [p[:, half:] for p in both_streams]
    put([out_cot], cot_value(pairs, weights, gain, both(own, other, 1, width)))


def ffn_kernel(*refs):
    hidden, weights, outs = refs[:NX], refs[NX : 2 * NX], refs[2 * NX :]
    times_down([h[...] for h in hidden], weights, outs)


def cot_out_kernel(own, other, gain, *refs):
    pairs, weights, outs = refs[:NX], refs[NX : 2 * NX], refs[2 * NX :]
    pairs = [p[...] for p in pairs]
    put(outs, cot_value(pairs, weights, gain, both(own, other, 2, gain.shape[-1])))


def final_kernel(where, base, hot0, hot1, *refs):
    pieces, out = refs[:NX], refs[NX]
    width = pieces[0].shape[-1]
    for d in range(NX):
        at = column_block(where[0] + NX - d, width)
        rows = base[:, at].astype(F32) + dot(hot0[...], pieces[d][0])
        rows = rows.astype(BF).astype(F32) + dot(hot1[...], pieces[d][1], (0, 0))
        out[:, at] = rows.astype(BF)


def back_x(deltas, xi):
    pieces = []
    for d in range(NX):
        part = lax.dynamic_slice_in_dim(deltas, ((xi + d) % NX) * CAP, CAP, 1)
        pieces.append(part if d == 0 else to_x(part, d))
    return pieces


def gather_x(block):
    return [block] + [to_x(block, d) for d in range(1, NX)]


def sum_parts(parts):
    return [parts[0]] + [to_x(parts[d], -d) for d in range(1, NX)]


def on_device(
    forward_in,
    entering,
    cotangent_in,
    cot_entering,
    stash,
    norm_gain,
    w_gate,
    w_up,
    w_down,
    ids_fwd,
    route_fwd,
    ids_bwd,
    route_bwd,
):
    section = lax.axis_index("section")
    last = lax.axis_size("section") - 1
    xi = lax.axis_index("x")
    zi = lax.axis_index("zh")
    depth = stash.shape[-1]
    width = depth // NX
    half = w_gate.shape[-1]
    rows = NZ * NX * CAP

    ids = jnp.concatenate([ids_fwd[:, 0], ids_bwd[:, 0]], axis=0)
    routes = jnp.concatenate([route_fwd[:, 0], route_bwd[:, 0]], axis=0)
    hot, mix = routing_plans(ids, routes, zi)
    own = lax.dynamic_index_in_dim(hot[:, 0], xi, 1, keepdims=False)
    flat = hot.reshape(4, rows, -1)

    where = xi.astype(jnp.int32).reshape(1)

    wide = [shape((3, CAP, width), BF)] * NX
    *first, hat1, word1 = kernel_call(
        pack_kernel,
        wide + [shape((CAP, depth), BF), shape((CAP, 128), F32)],
        [where, own, forward_in[0], stash[:, 0], cotangent_in[0]],
        smem_first=True,
        scratch=[
            pltpu.VMEM((3, CAP, depth), BF),
            pltpu.VMEM(forward_in.shape[1:], BF),
            pltpu.VMEM((2,) + forward_in.shape[1:], BF),
            pltpu.VMEM(forward_in.shape[1:], BF),
            pltpu.SemaphoreType.DMA((3,)),
        ],
        room=58,
        far=(2, 3, 4),
    )
    first = [first[0]] + [to_x(first[d], d) for d in range(1, NX)]

    weights = kernel_call(
        weights_kernel,
        [shape((width + width // 2, 2 * half), BF)] * NX,
        [after(w_gate[0, 0], hat1), w_up[0, 0], w_down[0, 0]],
        scratch=[pltpu.SemaphoreType.DMA((NX * (2 + width // (2 * half)),))],
        room=58,
        far=(0, 1, 2),
        far_out=True,
    )
    first[0] = after(first[0], weights[0])
    weights = [weights[0]] + [to_x(weights[d], d) for d in range(1, NX)]

    def in_order(pieces, sides, room=14):
        count, _, columns = pieces[0].shape
        outs = [shape((count, NX * CAP, columns), BF)] * sides
        return kernel_call(order_kernel, outs, [where] + pieces, smem_first=True, room=room)

    first_own = in_order(first, 1, 44)[0]
    first_other = to_other_z(first_own)

    gain = lax.dynamic_slice_in_dim(norm_gain, xi * width, width, 1)

    turned = jnp.swapaxes(flat, 1, 2)
    turned = after(turned, first_own)
    moved_fwd = to_section(jnp.concatenate([forward_in[0], turned[0]], axis=1), 1)
    moved_cot = to_section(jnp.concatenate([cotangent_in[0], turned[2]], axis=1), -1)
    base_fwd = jnp.where(section == 0, entering[0], moved_fwd[:, :depth])
    base_cot = jnp.where(section == last, cot_entering[0], moved_cot[:, :depth])
    hot_fwd, hot_cot = moved_fwd[:, depth:], moved_cot[:, depth:]
    later = kernel_call(
        pack_later_kernel,
        [shape((2, CAP, depth + 128), BF)],
        [own, base_fwd, base_cot, word1],
    )[0]
    later_far = to_other_z(after(later, first_other))

    def cross_x(hat1_far, *before):
        pieces = kernel_call(
            split_kernel,
            [shape((3, 2 * CAP, width + 128), BF)] * NX,
            [where, after(later, *before), later_far, hat1, hat1_far],
            smem_first=True,
        )
        return in_order([pieces[0]] + [to_x(pieces[d], d) for d in range(1, NX)], 2)

    group = jnp.arange(rows) // CAP
    same = (group[:, None] == group[None, :]).astype(F32)

    def carry(plan, before):
        move = (dot(flat[plan], before) * same).astype(BF)
        return jnp.concatenate([move, jnp.roll(move, NX * CAP, axis=1)], axis=1)

    carry_fwd = carry(1, hot_fwd)
    carry_cot = carry(3, hot_cot)
    own_fwd0 = lax.dynamic_slice_in_dim(hot_fwd, xi * CAP, CAP, 1)
    own_cot0 = lax.dynamic_slice_in_dim(hot_cot, xi * CAP, CAP, 1)

    def parts_of(kernel, operands, columns, count):
        outs = [shape((count, columns), F32)] + [shape((count, columns), BF)] * (NX - 1)
        return kernel_call(kernel, outs, operands)

    whole = [shape((rows, width), BF)]
    halves = [shape((NX * CAP, width), BF)] * 2

    parts = sum_parts(
        parts_of(
            first_kernel,
            [after(first_own, later_far), first_other, gain] + weights,
            2 * half,
            2 * rows + rows // 2,
        )
    )
    hat1_far = to_other_z(after(hat1, parts[0]))
    middle = [shape((rows, 4 * half), BF)]
    middle = kernel_call(middle_kernel, middle, [mix] + parts)[0]
    fwd0, cot0 = kernel_call(
        ends_kernel, whole * 2, [after(first_own, hat1_far), first_other, gain] + gather_x(middle) + weights
    )
    cot_crossed = to_section(cot0, -1, 1)
    cot_straight = to_section(cot0, -1)
    fwd_crossed = to_section(after(fwd0, cot_straight), 1, 1)
    fwd_straight = to_section(fwd0, 1)

    later_own, later_other = cross_x(hat1_far, fwd_straight, cot_straight)
    sums1 = sum_parts(
        parts_of(
            cot_next_kernel,
            [later_own, later_other, gain, carry_cot, cot_straight, cot_crossed] + weights,
            3 * half,
            rows,
        )
    )
    pair1 = kernel_call(pair_kernel, [shape((rows, 3 * half), BF)], [mix] + sums1)[0]
    next_pre = sum_parts(
        parts_of(
            pre_next_kernel,
            [later_own, later_other, gain, after(carry_fwd, pair1), fwd_straight, fwd_crossed]
            + weights,
            3 * half,
            rows,
        )
    )
    cot1 = kernel_call(
        cot_out_kernel, halves, [later_own, later_other, gain] + gather_x(pair1) + weights
    )
    hidden_kind = [shape((rows, half), BF)]
    hidden1 = kernel_call(functools.partial(hidden_kernel, depth), hidden_kind, [mix] + next_pre)[0]
    fwd1 = kernel_call(ffn_kernel, halves, gather_x(hidden1) + weights)

    def add_half(a, b):
        return (a.astype(F32) + b.astype(F32)).astype(BF)

    def finish(base, hot0, hot1, straight, crossed, now):
        count = NX * CAP
        before = add_half(straight[:count], crossed[count:])
        pieces = back_x(jnp.stack([before, add_half(now[0], to_other_z(now[1]))]), xi)
        out = [shape(base.shape, BF)]
        return kernel_call(final_kernel, out, [where, base, hot0, hot1] + pieces, smem_first=True)[0]

    cot_end = finish(base_cot, own_cot0, own[3], cot_straight, cot_crossed, cot1)
    fwd_end = finish(base_fwd, own_fwd0, own[1], fwd_straight, fwd_crossed, fwd1)
    return (fwd_end[None], cot_end[None])


def solution(mesh):
    split = Mesh(mesh.devices.reshape(-1, NX, NZ), ("section", "x", "zh"))
    expert = ("x", "zh")
    placed = (
        P("section", expert, None),
        P(None, expert, None),
        P("section", expert, None),
        P(None, expert, None),
        P(None, "section", expert, None),
        P("section", None),
        P("section", None, None, expert),
        P("section", None, None, expert),
        P("section", None, expert, None),
        P(None, "section", None, None),
        P(None, "section", None, None),
        P(None, "section", None, None),
        P(None, "section", None, None),
    )
    return jax.shard_map(
        on_device,
        mesh=split,
        in_specs=placed,
        out_specs=(P("section", expert, None), P("section", expert, None)),
        check_vma=False,
    )
```

```python
import functools

import jax
import jax.numpy as jnp
from jax import lax
from jax.experimental import pallas as pl
from jax.experimental.pallas import tpu as pltpu
from jax.sharding import Mesh, PartitionSpec as P

CAP = 16
NX = 4
NZ = 2
EPSILON = 1e-06
BF = jnp.bfloat16
F32 = jnp.float32


def dot(a, b, contract=(1, 0)):
    dims = (((contract[0],), (contract[1],)), ((), ()))
    return lax.dot_general(a, b, dims, preferred_element_type=F32)


def to_x(block, distance):
    route = [(i, (i + distance) % NX) for i in range(NX)]
    return lax.ppermute(block, "x", route)


def to_other_z(block):
    return lax.ppermute(block, "zh", [(0, 1), (1, 0)])


def to_section(block, step, flip=0):
    count = lax.axis_size("section")
    route = []
    for s in range(count):
        if 0 <= s + step < count:
            for z in range(NZ):
                route.append((s * NZ + z, (s + step) * NZ + (z ^ flip)))
    return lax.ppermute(block, ("section", "zh"), route)


def routing_plans(ids, weights, zi):
    plans = ids.shape[0]
    matches = (ids == 0).astype(F32)
    mixing = jnp.sum(weights * matches, axis=-1).reshape(plans, NX, NZ, -1)
    member = jnp.sum(matches, axis=-1).reshape(plans, NX, NZ, -1)
    rows = member.shape[-1]
    swap = lambda a: jnp.where(zi == 0, a, a[:, :, ::-1])
    mixing = jnp.transpose(swap(mixing), (0, 2, 1, 3))
    member = jnp.transpose(swap(member), (0, 2, 1, 3))
    upto = (lax.broadcasted_iota(jnp.int32, (rows, rows), 0) <= lax.broadcasted_iota(jnp.int32, (rows, rows), 1)).astype(BF)
    order = dot(member.reshape(-1, rows).astype(BF), upto).reshape(member.shape)
    slot = jnp.where(member > 0, order, 0.0)
    wanted = jnp.arange(1, CAP + 1, dtype=jnp.int32).astype(F32)
    one_hot = (slot[..., None, :] == wanted[:, None]).astype(F32)
    spread = jnp.broadcast_to(mixing[..., None, :], one_hot.shape)
    slot_weight = jnp.sum((one_hot * spread).reshape(plans, -1, rows), axis=-1, keepdims=True)
    return one_hot.astype(BF), slot_weight


def after(value, *before):
    return lax.optimization_barrier((value,) + before)[0]


def two_words(column):
    high = lax.reduce_precision(column, 8, 7)
    low = column - high
    lane = lax.broadcasted_iota(jnp.int32, (column.shape[0], 128), 1)
    return jnp.where(lane == 0, high, jnp.where(lane == 1, low, 0.0)).astype(BF)


def kernel_call(kernel, outs, operands, smem_first=False, scratch=(), room=14, far=(), far_out=False):
    specs = [
        pl.BlockSpec(memory_space=pl.ANY if i in far else pltpu.VMEM) for i in range(len(operands))
    ]
    if smem_first:
        specs[0] = pl.BlockSpec(memory_space=pltpu.SMEM)
    return pl.pallas_call(
        kernel,
        out_shape=outs,
        in_specs=specs,
        out_specs=[pl.BlockSpec(memory_space=pl.ANY if far_out else pltpu.VMEM) for _ in outs],
        scratch_shapes=list(scratch),
        cost_estimate=pl.CostEstimate(flops=1000, bytes_accessed=1000, transcendentals=0),
        compiler_params=pltpu.CompilerParams(vmem_limit_bytes=room * 2**20),
    )(*operands)


def shape(dims, dtype):
    return jax.ShapeDtypeStruct(dims, dtype)


def column_block(index, width):
    return pl.ds(pl.multiple_of(lax.rem(index, NX) * width, 128), width)


def pack_kernel(where, hot, fwd, stash, cot, *rest):
    outs, (hat1, word1, packed, near_fwd, near_stash, near_cot, sems) = rest[:NX], rest[NX:]
    copies = [
        pltpu.make_async_copy(fwd, near_fwd, sems.at[0]),
        pltpu.make_async_copy(stash, near_stash, sems.at[1]),
        pltpu.make_async_copy(cot, near_cot, sems.at[2]),
    ]
    for copy in copies:
        copy.start()
    for copy in copies:
        copy.wait()
    fwd, stash, cot = near_fwd, near_stash, near_cot
    width = outs[0].shape[-1]
    x_fwd = dot(hot[0], fwd[...])
    x_bwd = dot(hot[2], stash[0])
    x_next = dot(hot[3], stash[1])
    g = dot(hot[2], cot[...])

    def inverse(x):
        return lax.rsqrt(jnp.mean(x * x, axis=-1, keepdims=True) + EPSILON)

    inv0, inv1 = inverse(x_bwd), inverse(x_next)
    packed[0] = (x_fwd * inverse(x_fwd)).astype(BF)
    packed[1] = (x_bwd * inv0).astype(BF)
    packed[2] = (g * inv0).astype(BF)
    hat1[...] = (x_next * inv1).astype(BF)
    word1[...] = jnp.broadcast_to(inv1, word1.shape)
    for d in range(NX):
        outs[d][...] = packed[:, :, column_block(where[0] + d, width)]


def pack_later_kernel(hot, fwd, cot, word1, out):
    depth = fwd.shape[-1]
    inv1 = word1[:, :1]
    out[0, :, :depth] = dot(hot[1], fwd[...]).astype(BF)
    out[1, :, :depth] = (dot(hot[3], cot[...]) * inv1).astype(BF)
    words = two_words(inv1)
    for i in range(2):
        out[i, :, depth:] = words


def weights_kernel(gate, up, down, *refs):
    outs, sems = refs[:NX], refs[NX]
    width, half = gate.shape[0] // NX, gate.shape[1]
    me = lax.axis_index("x")
    copies = []

    def move(source, target):
        copies.append(pltpu.make_async_copy(source, target, sems.at[len(copies)]))
        copies[-1].start()

    for d in (1, 3, 2, 0):
        at = pl.multiple_of(lax.rem(me + d, NX) * width, 128)
        move(gate.at[pl.ds(at, width), :], outs[d].at[:width, :half])
        move(up.at[pl.ds(at, width), :], outs[d].at[:width, half:])
        for j in range(width // (2 * half)):
            to = width + j * half
            across = pl.ds(pl.multiple_of(at + j * 2 * half, 128), 2 * half)
            move(down.at[:, across], outs[d].at[to : to + half, :])
    for copy in copies:
        copy.wait()


def down_blocks(weights):
    wide = weights.shape[1]
    half = wide // 2
    blocks = weights.shape[0] // (wide + half)
    for j in range(blocks):
        to = blocks * wide + j * half
        yield slice(j * wide, (j + 1) * wide), slice(to, to + half)


def times_down(hidden, weights, outs):
    for columns, lines in down_blocks(weights[0]):
        value = sum(dot(h, w[lines, :]) for h, w in zip(hidden, weights))
        put(outs, value, columns)


def times_down_back(x, weights):
    return sum(dot(x[:, columns], weights[lines, :], (1, 1)) for columns, lines in down_blocks(weights))


def split_kernel(where, own, other, own_hat, other_hat, *outs):
    width = own_hat.shape[-1] // NX
    for d in range(NX):
        at = column_block(where[0] + d, width)
        for side, (rows, hat) in enumerate(((own, own_hat), (other, other_hat))):
            lines = slice(side * CAP, (side + 1) * CAP)
            outs[d][:2, lines, :width] = rows[:, :, at]
            outs[d][:2, lines, width:] = rows[:, :, NX * width :]
            outs[d][2, lines, :width] = hat[:, at]
            outs[d][2, lines, width:] = rows[1, :, NX * width :]


def order_kernel(where, *refs):
    pieces, outs = refs[:NX], refs[NX:]
    for d in range(NX):
        at = pl.multiple_of(lax.rem(where[0] + NX - d, NX) * CAP, CAP)
        for side, out in enumerate(outs):
            out[:, pl.ds(at, CAP), :] = pieces[d][:, side * CAP : (side + 1) * CAP, :]


def both(own, other, index, width):
    return jnp.concatenate([own[index, :, :width], other[index, :, :width]], axis=0)


def gained(x, gain):
    return (x.astype(F32) * gain[...]).astype(BF)


def first_kernel(own, other, gain, *refs):
    weights, outs = refs[:NX], refs[NX:]
    width = gain.shape[-1]
    x_fwd = gained(both(own, other, 0, width), gain)
    x_bwd = gained(both(own, other, 1, width), gain)
    cot = both(own, other, 2, width)
    rows = x_fwd.shape[0]
    for w, out in zip(weights, outs):
        out[:rows, :] = dot(x_fwd, w[:width, :]).astype(out.dtype)
        out[rows : 2 * rows, :] = dot(x_bwd, w[:width, :]).astype(out.dtype)
        hidden_cot = times_down_back(cot, w).astype(out.dtype)
        out[2 * rows :, : w.shape[1] // 2] = hidden_cot[: rows // 2]
        out[2 * rows :, w.shape[1] // 2 :] = hidden_cot[rows // 2 :]


def pre_next_kernel(own, other, gain, carry, straight, crossed, *refs):
    weights, outs = refs[:NX], refs[NX:]
    width, wide = gain.shape[-1], weights[0].shape[-1]
    count = straight.shape[0]
    x = both(own, other, 0, width).astype(F32)
    x = x + dot(carry[:, :count], straight[...]) + dot(carry[:, count:], crossed[...])
    squares = two_words(jnp.sum(x * x, axis=-1, keepdims=True))
    x = (x * gain[...]).astype(BF)
    for w, out in zip(weights, outs):
        out[:, :wide] = dot(x, w[:width, :]).astype(out.dtype)
        out[:, wide:] = squares.astype(out.dtype)


def cot_next_kernel(own, other, gain, carry, straight, crossed, *refs):
    weights, outs = refs[:NX], refs[NX:]
    width, count = straight.shape[-1], straight.shape[0]
    words = jnp.concatenate([own[1, :, width:], other[1, :, width:]], axis=0).astype(F32)
    inverse = words[:, :1] + words[:, 1:2]
    moved = dot(carry[:, :count], straight[...]) + dot(carry[:, count:], crossed[...])
    x = (both(own, other, 1, width).astype(F32) + inverse * moved).astype(BF)
    hat = gained(both(own, other, 2, width), gain)
    wide = weights[0].shape[-1]
    for w, out in zip(weights, outs):
        out[:, :wide] = dot(hat, w[:width, :]).astype(out.dtype)
        out[:, wide:] = times_down_back(x, w).astype(out.dtype)


def total(parts, rows=slice(None), columns=slice(None)):
    return sum(p[rows, columns].astype(F32) for p in parts)


def hidden_of(gate, up, mix):
    return (gate * jax.nn.sigmoid(gate) * up * mix).astype(BF)


def pair_of(hidden_cot, gate, up):
    sigma = jax.nn.sigmoid(gate)
    gate_cot = hidden_cot * up * sigma * (1.0 + gate * (1.0 - sigma))
    up_cot = hidden_cot * gate * sigma
    along = gate_cot * gate + up_cot * up
    return jnp.concatenate([gate_cot, up_cot, along], axis=1).astype(BF)


def middle_kernel(mix, *refs):
    parts, out = refs[:NX], refs[NX]
    count, half = out.shape[0], parts[0].shape[1] // 2
    pre = total(parts)
    hidden_cot = pre[2 * count :]
    hidden_cot = jnp.concatenate([hidden_cot[:, :half], hidden_cot[:, half:]], axis=0)
    out[:, :half] = hidden_of(pre[:count, :half], pre[:count, half:], mix[0])
    out[:, half:] = pair_of(
        hidden_cot * mix[2], pre[count : 2 * count, :half], pre[count : 2 * count, half:]
    )


def hidden_kernel(depth, mix, *refs):
    parts, out = refs[:NX], refs[NX]
    half = out.shape[1]
    pre = total(parts)
    words = pre[:, 2 * half :]
    scale = lax.rsqrt((words[:, :1] + words[:, 1:2]) / depth + EPSILON)
    out[...] = hidden_of(pre[:, :half] * scale, pre[:, half : 2 * half] * scale, mix[1])


def pair_kernel(mix, *refs):
    parts, out = refs[:NX], refs[NX]
    half = out.shape[1] // 3
    pre = total(parts)
    out[...] = pair_of(pre[:, 2 * half :] * mix[3], pre[:, :half], pre[:, half : 2 * half])


def put(outs, value, columns=slice(None)):
    at = 0
    for out in outs:
        out[:, columns] = value[at : at + out.shape[0]].astype(out.dtype)
        at += out.shape[0]


def cot_value(pairs, weights, gain, hat):
    width, wide = gain.shape[-1], weights[0].shape[-1]
    normed_cot = sum(dot(p[:, :wide], w[:width, :], (1, 1)) for p, w in zip(pairs, weights))
    along = sum(p[:, wide:].astype(F32) for p in pairs)
    along = jnp.sum(along, axis=-1, keepdims=True) / (NX * width)
    return normed_cot * gain[...] - hat.astype(F32) * along


def ends_kernel(own, other, gain, *refs):
    both_streams, weights, (out_fwd, out_cot) = refs[:NX], refs[NX : 2 * NX], refs[2 * NX :]
    half, width = weights[0].shape[-1] // 2, gain.shape[-1]
    times_down([p[:, :half] for p in both_streams], weights, [out_fwd])
    pairs = [p[:, half:] for p in both_streams]
    put([out_cot], cot_value(pairs, weights, gain, both(own, other, 1, width)))


def ffn_kernel(*refs):
    hidden, weights, outs = refs[:NX], refs[NX : 2 * NX], refs[2 * NX :]
    times_down([h[...] for h in hidden], weights, outs)


def cot_out_kernel(own, other, gain, *refs):
    pairs, weights, outs = refs[:NX], refs[NX : 2 * NX], refs[2 * NX :]
    pairs = [p[...] for p in pairs]
    put(outs, cot_value(pairs, weights, gain, both(own, other, 2, gain.shape[-1])))


def final_kernel(where, base, hot0, hot1, *refs):
    pieces, out = refs[:NX], refs[NX]
    width = pieces[0].shape[-1]
    for d in range(NX):
        at = column_block(where[0] + NX - d, width)
        rows = base[:, at].astype(F32) + dot(hot0[...], pieces[d][0])
        rows = rows.astype(BF).astype(F32) + dot(hot1[...], pieces[d][1], (0, 0))
        out[:, at] = rows.astype(BF)


def back_x(deltas, xi):
    pieces = []
    for d in range(NX):
        part = lax.dynamic_slice_in_dim(deltas, ((xi + d) % NX) * CAP, CAP, 1)
        pieces.append(part if d == 0 else to_x(part, d))
    return pieces


def gather_x(block):
    return [block] + [to_x(block, d) for d in range(1, NX)]


def sum_parts(parts):
    return [parts[0]] + [to_x(parts[d], -d) for d in range(1, NX)]


def on_device(
    forward_in,
    entering,
    cotangent_in,
    cot_entering,
    stash,
    norm_gain,
    w_gate,
    w_up,
    w_down,
    ids_fwd,
    route_fwd,
    ids_bwd,
    route_bwd,
):
    section = lax.axis_index("section")
    last = lax.axis_size("section") - 1
    xi = lax.axis_index("x")
    zi = lax.axis_index("zh")
    depth = stash.shape[-1]
    width = depth // NX
    half = w_gate.shape[-1]
    rows = NZ * NX * CAP

    ids = jnp.concatenate([ids_fwd[:, 0], ids_bwd[:, 0]], axis=0)
    routes = jnp.concatenate([route_fwd[:, 0], route_bwd[:, 0]], axis=0)
    hot, mix = routing_plans(ids, routes, zi)
    own = lax.dynamic_index_in_dim(hot[:, 0], xi, 1, keepdims=False)
    flat = hot.reshape(4, rows, -1)

    where = xi.astype(jnp.int32).reshape(1)

    wide = [shape((3, CAP, width), BF)] * NX
    *first, hat1, word1 = kernel_call(
        pack_kernel,
        wide + [shape((CAP, depth), BF), shape((CAP, 128), F32)],
        [where, own, forward_in[0], stash[:, 0], cotangent_in[0]],
        smem_first=True,
        scratch=[
            pltpu.VMEM((3, CAP, depth), BF),
            pltpu.VMEM(forward_in.shape[1:], BF),
            pltpu.VMEM((2,) + forward_in.shape[1:], BF),
            pltpu.VMEM(forward_in.shape[1:], BF),
            pltpu.SemaphoreType.DMA((3,)),
        ],
        room=58,
        far=(2, 3, 4),
    )
    first = [first[0]] + [to_x(first[d], d) for d in range(1, NX)]

    weights = kernel_call(
        weights_kernel,
        [shape((width + width // 2, 2 * half), BF)] * NX,
        [after(w_gate[0, 0], hat1), w_up[0, 0], w_down[0, 0]],
        scratch=[pltpu.SemaphoreType.DMA((NX * (2 + width // (2 * half)),))],
        room=58,
        far=(0, 1, 2),
    )
    first[0] = after(first[0], weights[0])
    weights = [weights[0]] + [to_x(weights[d], d) for d in range(1, NX)]

    def in_order(pieces, sides, room=14):
        count, _, columns = pieces[0].shape
        outs = [shape((count, NX * CAP, columns), BF)] * sides
        return kernel_call(order_kernel, outs, [where] + pieces, smem_first=True, room=room)

    first_own = in_order(first, 1, 44)[0]
    first_other = to_other_z(first_own)

    gain = lax.dynamic_slice_in_dim(norm_gain, xi * width, width, 1)

    turned = jnp.swapaxes(flat, 1, 2)
    moved_fwd = to_section(jnp.concatenate([forward_in[0], turned[0]], axis=1), 1)
    moved_cot = to_section(jnp.concatenate([cotangent_in[0], turned[2]], axis=1), -1)
    base_fwd = jnp.where(section == 0, entering[0], moved_fwd[:, :depth])
    base_cot = jnp.where(section == last, cot_entering[0], moved_cot[:, :depth])
    hot_fwd, hot_cot = moved_fwd[:, depth:], moved_cot[:, depth:]
    later = kernel_call(
        pack_later_kernel,
        [shape((2, CAP, depth + 128), BF)],
        [own, base_fwd, base_cot, word1],
    )[0]
    later_far = to_other_z(after(later, first_other))

    def cross_x(hat1_far, *before):
        pieces = kernel_call(
            split_kernel,
            [shape((3, 2 * CAP, width + 128), BF)] * NX,
            [where, after(later, *before), later_far, hat1, hat1_far],
            smem_first=True,
        )
        return in_order([pieces[0]] + [to_x(pieces[d], d) for d in range(1, NX)], 2)

    group = jnp.arange(rows) // CAP
    same = (group[:, None] == group[None, :]).astype(F32)

    def carry(plan, before):
        move = (dot(flat[plan], before) * same).astype(BF)
        return jnp.concatenate([move, jnp.roll(move, NX * CAP, axis=1)], axis=1)

    carry_fwd = carry(1, hot_fwd)
    carry_cot = carry(3, hot_cot)
    own_fwd0 = lax.dynamic_slice_in_dim(hot_fwd, xi * CAP, CAP, 1)
    own_cot0 = lax.dynamic_slice_in_dim(hot_cot, xi * CAP, CAP, 1)

    def parts_of(kernel, operands, columns, count):
        outs = [shape((count, columns), F32)] + [shape((count, columns), BF)] * (NX - 1)
        return kernel_call(kernel, outs, operands)

    whole = [shape((rows, width), BF)]
    halves = [shape((NX * CAP, width), BF)] * 2

    parts = sum_parts(
        parts_of(
            first_kernel,
            [after(first_own, later_far), first_other, gain] + weights,
            2 * half,
            2 * rows + rows // 2,
        )
    )
    hat1_far = to_other_z(after(hat1, parts[0]))
    middle = [shape((rows, 4 * half), BF)]
    middle = kernel_call(middle_kernel, middle, [mix] + parts)[0]
    fwd0, cot0 = kernel_call(
        ends_kernel, whole * 2, [after(first_own, hat1_far), first_other, gain] + gather_x(middle) + weights
    )
    cot_crossed = to_section(cot0, -1, 1)
    cot_straight = to_section(cot0, -1)
    fwd_crossed = to_section(fwd0, 1, 1)
    fwd_straight = to_section(fwd0, 1)

    later_own, later_other = cross_x(hat1_far, cot0)
    sums1 = sum_parts(
        parts_of(
            cot_next_kernel,
            [later_own, later_other, gain, carry_cot, cot_straight, cot_crossed] + weights,
            3 * half,
            rows,
        )
    )
    pair1 = kernel_call(pair_kernel, [shape((rows, 3 * half), BF)], [mix] + sums1)[0]
    cot1 = kernel_call(
        cot_out_kernel, halves, [later_own, later_other, gain] + gather_x(pair1) + weights
    )
    next_pre = sum_parts(
        parts_of(
            pre_next_kernel,
            [later_own, later_other, gain, after(carry_fwd, cot1[0]), fwd_straight, fwd_crossed]
            + weights,
            3 * half,
            rows,
        )
    )
    hidden_kind = [shape((rows, half), BF)]
    hidden1 = kernel_call(functools.partial(hidden_kernel, depth), hidden_kind, [mix] + next_pre)[0]
    fwd1 = kernel_call(ffn_kernel, halves, gather_x(hidden1) + weights)

    def add_half(a, b):
        return (a.astype(F32) + b.astype(F32)).astype(BF)

    def finish(base, hot0, hot1, straight, crossed, now):
        count = NX * CAP
        before = add_half(straight[:count], crossed[count:])
        pieces = back_x(jnp.stack([before, add_half(now[0], to_other_z(now[1]))]), xi)
        out = [shape(base.shape, BF)]
        return kernel_call(final_kernel, out, [where, base, hot0, hot1] + pieces, smem_first=True)[0]

    cot_end = finish(base_cot, own_cot0, own[3], cot_straight, cot_crossed, cot1)
    fwd_end = finish(base_fwd, own_fwd0, own[1], fwd_straight, fwd_crossed, fwd1)
    return (fwd_end[None], cot_end[None])


def solution(mesh):
    split = Mesh(mesh.devices.reshape(-1, NX, NZ), ("section", "x", "zh"))
    expert = ("x", "zh")
    placed = (
        P("section", expert, None),
        P(None, expert, None),
        P("section", expert, None),
        P(None, expert, None),
        P(None, "section", expert, None),
        P("section", None),
        P("section", None, None, expert),
        P("section", None, None, expert),
        P("section", None, expert, None),
        P(None, "section", None, None),
        P(None, "section", None, None),
        P(None, "section", None, None),
        P(None, "section", None, None),
    )
    return jax.shard_map(
        on_device,
        mesh=split,
        in_specs=placed,
        out_specs=(P("section", expert, None), P("section", expert, None)),
        check_vma=False,
    )
```

```python
import functools

import jax
import jax.numpy as jnp
from jax import lax
from jax.experimental import pallas as pl
from jax.experimental.pallas import tpu as pltpu
from jax.sharding import Mesh, PartitionSpec as P

CAP = 16
NX = 4
NZ = 2
EPSILON = 1e-06
BF = jnp.bfloat16
F32 = jnp.float32


def dot(a, b, contract=(1, 0)):
    dims = (((contract[0],), (contract[1],)), ((), ()))
    return lax.dot_general(a, b, dims, preferred_element_type=F32)


def to_x(block, distance):
    route = [(i, (i + distance) % NX) for i in range(NX)]
    return lax.ppermute(block, "x", route)


def to_other_z(block):
    return lax.ppermute(block, "zh", [(0, 1), (1, 0)])


def to_section(block, step):
    count = lax.axis_size("section")
    route = [(s, s + step) for s in range(count) if 0 <= s + step < count]
    return lax.ppermute(block, "section", route)


def routing_plans(ids, weights, zi):
    plans = ids.shape[0]
    matches = (ids == 0).astype(F32)
    mixing = jnp.sum(weights * matches, axis=-1).reshape(plans, NX, NZ, -1)
    member = jnp.sum(matches, axis=-1).reshape(plans, NX, NZ, -1)
    rows = member.shape[-1]
    swap = lambda a: jnp.where(zi == 0, a, a[:, :, ::-1])
    mixing = jnp.transpose(swap(mixing), (0, 2, 1, 3))
    member = jnp.transpose(swap(member), (0, 2, 1, 3))
    upto = (lax.broadcasted_iota(jnp.int32, (rows, rows), 0) <= lax.broadcasted_iota(jnp.int32, (rows, rows), 1)).astype(BF)
    order = dot(member.reshape(-1, rows).astype(BF), upto).reshape(member.shape)
    slot = jnp.where(member > 0, order, 0.0)
    wanted = jnp.arange(1, CAP + 1, dtype=jnp.int32).astype(F32)
    one_hot = (slot[..., None, :] == wanted[:, None]).astype(F32)
    spread = jnp.broadcast_to(mixing[..., None, :], one_hot.shape)
    slot_weight = jnp.sum((one_hot * spread).reshape(plans, -1, rows), axis=-1, keepdims=True)
    return one_hot.astype(BF), slot_weight


def after(value, *before):
    return lax.optimization_barrier((value,) + before)[0]


def two_words(column):
    high = lax.reduce_precision(column, 8, 7)
    low = column - high
    lane = lax.broadcasted_iota(jnp.int32, (column.shape[0], 128), 1)
    return jnp.where(lane == 0, high, jnp.where(lane == 1, low, 0.0)).astype(BF)


def kernel_call(kernel, outs, operands, smem_first=False, scratch=(), room=14, far=(), far_out=False):
    specs = [
        pl.BlockSpec(memory_space=pl.ANY if i in far else pltpu.VMEM) for i in range(len(operands))
    ]
    if smem_first:
        specs[0] = pl.BlockSpec(memory_space=pltpu.SMEM)
    return pl.pallas_call(
        kernel,
        out_shape=outs,
        in_specs=specs,
        out_specs=[pl.BlockSpec(memory_space=pl.ANY if far_out else pltpu.VMEM) for _ in outs],
        scratch_shapes=list(scratch),
        cost_estimate=pl.CostEstimate(flops=1000, bytes_accessed=1000, transcendentals=0),
        compiler_params=pltpu.CompilerParams(vmem_limit_bytes=room * 2**20),
    )(*operands)


def shape(dims, dtype):
    return jax.ShapeDtypeStruct(dims, dtype)


def column_block(index, width):
    return pl.ds(pl.multiple_of(lax.rem(index, NX) * width, 128), width)


def pack_kernel(where, hot, fwd, stash, cot, *rest):
    outs, (hat1, word1, packed, near_fwd, near_stash, near_cot, sems) = rest[:NX], rest[NX:]
    copies = [
        pltpu.make_async_copy(fwd, near_fwd, sems.at[0]),
        pltpu.make_async_copy(stash, near_stash, sems.at[1]),
        pltpu.make_async_copy(cot, near_cot, sems.at[2]),
    ]
    for copy in copies:
        copy.start()
    for copy in copies:
        copy.wait()
    fwd, stash, cot = near_fwd, near_stash, near_cot
    width = outs[0].shape[-1]
    x_fwd = dot(hot[0], fwd[...])
    x_bwd = dot(hot[2], stash[0])
    x_next = dot(hot[3], stash[1])
    g = dot(hot[2], cot[...])

    def inverse(x):
        return lax.rsqrt(jnp.mean(x * x, axis=-1, keepdims=True) + EPSILON)

    inv0, inv1 = inverse(x_bwd), inverse(x_next)
    packed[0] = (x_fwd * inverse(x_fwd)).astype(BF)
    packed[1] = (x_bwd * inv0).astype(BF)
    packed[2] = (g * inv0).astype(BF)
    hat1[...] = (x_next * inv1).astype(BF)
    word1[...] = jnp.broadcast_to(inv1, word1.shape)
    for d in range(NX):
        outs[d][...] = packed[:, :, column_block(where[0] + d, width)]


def pack_later_kernel(hot, fwd, cot, word1, out):
    depth = fwd.shape[-1]
    inv1 = word1[:, :1]
    out[0, :, :depth] = dot(hot[1], fwd[...]).astype(BF)
    out[1, :, :depth] = (dot(hot[3], cot[...]) * inv1).astype(BF)
    words = two_words(inv1)
    for i in range(2):
        out[i, :, depth:] = words


def weights_kernel(gate, up, down, *refs):
    outs, sems = refs[:NX], refs[NX]
    width, half = gate.shape[0] // NX, gate.shape[1]
    me = lax.axis_index("x")
    copies = []

    def move(source, target):
        copies.append(pltpu.make_async_copy(source, target, sems.at[len(copies)]))
        copies[-1].start()

    for d in (1, 3, 2, 0):
        at = pl.multiple_of(lax.rem(me + d, NX) * width, 128)
        move(gate.at[pl.ds(at, width), :], outs[d].at[:width, :half])
        move(up.at[pl.ds(at, width), :], outs[d].at[:width, half:])
        for j in range(width // (2 * half)):
            to = width + j * half
            across = pl.ds(pl.multiple_of(at + j * 2 * half, 128), 2 * half)
            move(down.at[:, across], outs[d].at[to : to + half, :])
    for copy in copies:
        copy.wait()


def down_blocks(weights):
    wide = weights.shape[1]
    half = wide // 2
    blocks = weights.shape[0] // (wide + half)
    for j in range(blocks):
        to = blocks * wide + j * half
        yield slice(j * wide, (j + 1) * wide), slice(to, to + half)


def times_down(hidden, weights, outs):
    for columns, lines in down_blocks(weights[0]):
        value = sum(dot(h, w[lines, :]) for h, w in zip(hidden, weights))
        put(outs, value, columns)


def times_down_back(x, weights):
    return sum(dot(x[:, columns], weights[lines, :], (1, 1)) for columns, lines in down_blocks(weights))


def split_kernel(where, own, other, own_hat, other_hat, *outs):
    width = own_hat.shape[-1] // NX
    for d in range(NX):
        at = column_block(where[0] + d, width)
        for side, (rows, hat) in enumerate(((own, own_hat), (other, other_hat))):
            lines = slice(side * CAP, (side + 1) * CAP)
            outs[d][:2, lines, :width] = rows[:, :, at]
            outs[d][:2, lines, width:] = rows[:, :, NX * width :]
            outs[d][2, lines, :width] = hat[:, at]
            outs[d][2, lines, width:] = rows[1, :, NX * width :]


def order_kernel(where, *refs):
    pieces, outs = refs[:NX], refs[NX:]
    for d in range(NX):
        at = pl.multiple_of(lax.rem(where[0] + NX - d, NX) * CAP, CAP)
        for side, out in enumerate(outs):
            out[:, pl.ds(at, CAP), :] = pieces[d][:, side * CAP : (side + 1) * CAP, :]


def both(own, other, index, width):
    return jnp.concatenate([own[index, :, :width], other[index, :, :width]], axis=0)


def gained(x, gain):
    return (x.astype(F32) * gain[...]).astype(BF)


def first_kernel(own, other, gain, *refs):
    weights, outs = refs[:NX], refs[NX:]
    width = gain.shape[-1]
    x_fwd = gained(both(own, other, 0, width), gain)
    x_bwd = gained(both(own, other, 1, width), gain)
    cot = both(own, other, 2, width)
    rows = x_fwd.shape[0]
    for w, out in zip(weights, outs):
        out[:rows, :] = dot(x_fwd, w[:width, :]).astype(out.dtype)
        out[rows : 2 * rows, :] = dot(x_bwd, w[:width, :]).astype(out.dtype)
        hidden_cot = times_down_back(cot, w).astype(out.dtype)
        out[2 * rows :, : w.shape[1] // 2] = hidden_cot[: rows // 2]
        out[2 * rows :, w.shape[1] // 2 :] = hidden_cot[rows // 2 :]


def pre_next_kernel(own, other, gain, carry, straight, crossed, *refs):
    weights, outs = refs[:NX], refs[NX:]
    width, wide = gain.shape[-1], weights[0].shape[-1]
    count = straight.shape[0]
    x = both(own, other, 0, width).astype(F32)
    x = x + dot(carry[:, :count], straight[...]) + dot(carry[:, count:], crossed[...])
    squares = two_words(jnp.sum(x * x, axis=-1, keepdims=True))
    x = (x * gain[...]).astype(BF)
    for w, out in zip(weights, outs):
        out[:, :wide] = dot(x, w[:width, :]).astype(out.dtype)
        out[:, wide:] = squares.astype(out.dtype)


def cot_next_kernel(own, other, gain, carry, straight, crossed, *refs):
    weights, outs = refs[:NX], refs[NX:]
    width, count = straight.shape[-1], straight.shape[0]
    words = jnp.concatenate([own[1, :, width:], other[1, :, width:]], axis=0).astype(F32)
    inverse = words[:, :1] + words[:, 1:2]
    moved = dot(carry[:, :count], straight[...]) + dot(carry[:, count:], crossed[...])
    x = (both(own, other, 1, width).astype(F32) + inverse * moved).astype(BF)
    hat = gained(both(own, other, 2, width), gain)
    wide = weights[0].shape[-1]
    for w, out in zip(weights, outs):
        out[:, :wide] = dot(hat, w[:width, :]).astype(out.dtype)
        out[:, wide:] = times_down_back(x, w).astype(out.dtype)


def total(parts, rows=slice(None), columns=slice(None)):
    return sum(p[rows, columns].astype(F32) for p in parts)


def hidden_of(gate, up, mix):
    return (gate * jax.nn.sigmoid(gate) * up * mix).astype(BF)


def pair_of(hidden_cot, gate, up):
    sigma = jax.nn.sigmoid(gate)
    gate_cot = hidden_cot * up * sigma * (1.0 + gate * (1.0 - sigma))
    up_cot = hidden_cot * gate * sigma
    along = gate_cot * gate + up_cot * up
    return jnp.concatenate([gate_cot, up_cot, along], axis=1).astype(BF)


def middle_kernel(mix, *refs):
    parts, out = refs[:NX], refs[NX]
    count, half = out.shape[0], parts[0].shape[1] // 2
    pre = total(parts)
    hidden_cot = pre[2 * count :]
    hidden_cot = jnp.concatenate([hidden_cot[:, :half], hidden_cot[:, half:]], axis=0)
    out[:, :half] = hidden_of(pre[:count, :half], pre[:count, half:], mix[0])
    out[:, half:] = pair_of(
        hidden_cot * mix[2], pre[count : 2 * count, :half], pre[count : 2 * count, half:]
    )


def hidden_kernel(depth, mix, *refs):
    parts, out = refs[:NX], refs[NX]
    half = out.shape[1]
    pre = total(parts)
    words = pre[:, 2 * half :]
    scale = lax.rsqrt((words[:, :1] + words[:, 1:2]) / depth + EPSILON)
    out[...] = hidden_of(pre[:, :half] * scale, pre[:, half : 2 * half] * scale, mix[1])


def pair_kernel(mix, *refs):
    parts, out = refs[:NX], refs[NX]
    half = out.shape[1] // 3
    pre = total(parts)
    out[...] = pair_of(pre[:, 2 * half :] * mix[3], pre[:, :half], pre[:, half : 2 * half])


def put(outs, value, columns=slice(None)):
    at = 0
    for out in outs:
        out[:, columns] = value[at : at + out.shape[0]].astype(out.dtype)
        at += out.shape[0]


def cot_value(pairs, weights, gain, hat):
    width, wide = gain.shape[-1], weights[0].shape[-1]
    normed_cot = sum(dot(p[:, :wide], w[:width, :], (1, 1)) for p, w in zip(pairs, weights))
    along = sum(p[:, wide:].astype(F32) for p in pairs)
    along = jnp.sum(along, axis=-1, keepdims=True) / (NX * width)
    return normed_cot * gain[...] - hat.astype(F32) * along


def ends_kernel(own, other, gain, *refs):
    both_streams, weights, (out_fwd, out_cot) = refs[:NX], refs[NX : 2 * NX], refs[2 * NX :]
    half, width = weights[0].shape[-1] // 2, gain.shape[-1]
    times_down([p[:, :half] for p in both_streams], weights, [out_fwd])
    pairs = [p[:, half:] for p in both_streams]
    put([out_cot], cot_value(pairs, weights, gain, both(own, other, 1, width)))


def ffn_kernel(*refs):
    hidden, weights, outs = refs[:NX], refs[NX : 2 * NX], refs[2 * NX :]
    times_down([h[...] for h in hidden], weights, outs)


def cot_out_kernel(own, other, gain, *refs):
    pairs, weights, outs = refs[:NX], refs[NX : 2 * NX], refs[2 * NX :]
    pairs = [p[...] for p in pairs]
    put(outs, cot_value(pairs, weights, gain, both(own, other, 2, gain.shape[-1])))


def final_kernel(where, base, hot0, hot1, *refs):
    pieces, out = refs[:NX], refs[NX]
    width = pieces[0].shape[-1]
    for d in range(NX):
        at = column_block(where[0] + NX - d, width)
        rows = base[:, at].astype(F32) + dot(hot0[...], pieces[d][0])
        rows = rows.astype(BF).astype(F32) + dot(hot1[...], pieces[d][1], (0, 0))
        out[:, at] = rows.astype(BF)


def back_x(deltas, xi):
    pieces = []
    for d in range(NX):
        part = lax.dynamic_slice_in_dim(deltas, ((xi + d) % NX) * CAP, CAP, 1)
        pieces.append(part if d == 0 else to_x(part, d))
    return pieces


def gather_x(block):
    return [block] + [to_x(block, d) for d in range(1, NX)]


def sum_parts(parts):
    return [parts[0]] + [to_x(parts[d], -d) for d in range(1, NX)]


def on_device(
    forward_in,
    entering,
    cotangent_in,
    cot_entering,
    stash,
    norm_gain,
    w_gate,
    w_up,
    w_down,
    ids_fwd,
    route_fwd,
    ids_bwd,
    route_bwd,
):
    section = lax.axis_index("section")
    last = lax.axis_size("section") - 1
    xi = lax.axis_index("x")
    zi = lax.axis_index("zh")
    depth = stash.shape[-1]
    width = depth // NX
    half = w_gate.shape[-1]
    rows = NZ * NX * CAP

    ids = jnp.concatenate([ids_fwd[:, 0], ids_bwd[:, 0]], axis=0)
    routes = jnp.concatenate([route_fwd[:, 0], route_bwd[:, 0]], axis=0)
    hot, mix = routing_plans(ids, routes, zi)
    own = lax.dynamic_index_in_dim(hot[:, 0], xi, 1, keepdims=False)
    flat = hot.reshape(4, rows, -1)

    where = xi.astype(jnp.int32).reshape(1)

    wide = [shape((3, CAP, width), BF)] * NX
    *first, hat1, word1 = kernel_call(
        pack_kernel,
        wide + [shape((CAP, depth), BF), shape((CAP, 128), F32)],
        [where, own, forward_in[0], stash[:, 0], cotangent_in[0]],
        smem_first=True,
        scratch=[
            pltpu.VMEM((3, CAP, depth), BF),
            pltpu.VMEM(forward_in.shape[1:], BF),
            pltpu.VMEM((2,) + forward_in.shape[1:], BF),
            pltpu.VMEM(forward_in.shape[1:], BF),
            pltpu.SemaphoreType.DMA((3,)),
        ],
        room=58,
        far=(2, 3, 4),
    )
    first = [first[0]] + [to_x(first[d], d) for d in range(1, NX)]

    weights = kernel_call(
        weights_kernel,
        [shape((width + width // 2, 2 * half), BF)] * NX,
        [after(w_gate[0, 0], hat1), w_up[0, 0], w_down[0, 0]],
        scratch=[pltpu.SemaphoreType.DMA((NX * (2 + width // (2 * half)),))],
        room=58,
        far=(0, 1, 2),
    )
    first[0] = after(first[0], weights[0])
    weights = [weights[0]] + [to_x(weights[d], d) for d in range(1, NX)]

    def in_order(pieces, sides, room=14):
        count, _, columns = pieces[0].shape
        outs = [shape((count, NX * CAP, columns), BF)] * sides
        return kernel_call(order_kernel, outs, [where] + pieces, smem_first=True, room=room)

    first_own = in_order(first, 1, 44)[0]
    first_other = to_other_z(first_own)

    gain = lax.dynamic_slice_in_dim(norm_gain, xi * width, width, 1)

    turned = jnp.swapaxes(flat, 1, 2)
    moved_fwd = to_section(jnp.concatenate([forward_in[0], turned[0]], axis=1), 1)
    moved_cot = to_section(jnp.concatenate([cotangent_in[0], turned[2]], axis=1), -1)
    base_fwd = jnp.where(section == 0, entering[0], moved_fwd[:, :depth])
    base_cot = jnp.where(section == last, cot_entering[0], moved_cot[:, :depth])
    hot_fwd, hot_cot = moved_fwd[:, depth:], moved_cot[:, depth:]
    later = kernel_call(
        pack_later_kernel,
        [shape((2, CAP, depth + 128), BF)],
        [own, base_fwd, base_cot, word1],
    )[0]
    later_far = to_other_z(after(later, first_other))

    def cross_x(hat1_far, *before):
        pieces = kernel_call(
            split_kernel,
            [shape((3, 2 * CAP, width + 128), BF)] * NX,
            [where, after(later, *before), later_far, hat1, hat1_far],
            smem_first=True,
        )
        return in_order([pieces[0]] + [to_x(pieces[d], d) for d in range(1, NX)], 2)

    group = jnp.arange(rows) // CAP
    same = (group[:, None] == group[None, :]).astype(F32)

    def carry(plan, before):
        move = (dot(flat[plan], before) * same).astype(BF)
        return jnp.concatenate([move, jnp.roll(move, NX * CAP, axis=1)], axis=1)

    carry_fwd = carry(1, hot_fwd)
    carry_cot = carry(3, hot_cot)
    own_fwd0 = lax.dynamic_slice_in_dim(hot_fwd, xi * CAP, CAP, 1)
    own_cot0 = lax.dynamic_slice_in_dim(hot_cot, xi * CAP, CAP, 1)

    def parts_of(kernel, operands, columns, count):
        outs = [shape((count, columns), F32)] + [shape((count, columns), BF)] * (NX - 1)
        return kernel_call(kernel, outs, operands)

    whole = [shape((rows, width), BF)]
    halves = [shape((NX * CAP, width), BF)] * 2

    parts = sum_parts(
        parts_of(
            first_kernel,
            [after(first_own, later_far), first_other, gain] + weights,
            2 * half,
            2 * rows + rows // 2,
        )
    )
    hat1_far = to_other_z(after(hat1, parts[0]))
    middle = [shape((rows, 4 * half), BF)]
    middle = kernel_call(middle_kernel, middle, [mix] + parts)[0]
    fwd0, cot0 = kernel_call(
        ends_kernel, whole * 2, [after(first_own, hat1_far), first_other, gain] + gather_x(middle) + weights
    )
    cot_straight = to_section(cot0, -1)
    cot_crossed = to_other_z(cot_straight)
    fwd_straight = to_section(fwd0, 1)
    fwd_crossed = to_other_z(fwd_straight)

    later_own, later_other = cross_x(hat1_far, cot0)
    sums1 = sum_parts(
        parts_of(
            cot_next_kernel,
            [later_own, later_other, gain, carry_cot, cot_straight, cot_crossed] + weights,
            3 * half,
            rows,
        )
    )
    pair1 = kernel_call(pair_kernel, [shape((rows, 3 * half), BF)], [mix] + sums1)[0]
    cot1 = kernel_call(
        cot_out_kernel, halves, [later_own, later_other, gain] + gather_x(pair1) + weights
    )
    next_pre = sum_parts(
        parts_of(
            pre_next_kernel,
            [later_own, later_other, gain, after(carry_fwd, cot1[0]), fwd_straight, fwd_crossed]
            + weights,
            3 * half,
            rows,
        )
    )
    hidden_kind = [shape((rows, half), BF)]
    hidden1 = kernel_call(functools.partial(hidden_kernel, depth), hidden_kind, [mix] + next_pre)[0]
    fwd1 = kernel_call(ffn_kernel, halves, gather_x(hidden1) + weights)

    def add_half(a, b):
        return (a.astype(F32) + b.astype(F32)).astype(BF)

    def finish(base, hot0, hot1, straight, crossed, now):
        count = NX * CAP
        before = add_half(straight[:count], crossed[count:])
        pieces = back_x(jnp.stack([before, add_half(now[0], to_other_z(now[1]))]), xi)
        out = [shape(base.shape, BF)]
        return kernel_call(final_kernel, out, [where, base, hot0, hot1] + pieces, smem_first=True)[0]

    cot_end = finish(base_cot, own_cot0, own[3], cot_straight, cot_crossed, cot1)
    fwd_end = finish(base_fwd, own_fwd0, own[1], fwd_straight, fwd_crossed, fwd1)
    return (fwd_end[None], cot_end[None])


def solution(mesh):
    split = Mesh(mesh.devices.reshape(-1, NX, NZ), ("section", "x", "zh"))
    expert = ("x", "zh")
    placed = (
        P("section", expert, None),
        P(None, expert, None),
        P("section", expert, None),
        P(None, expert, None),
        P(None, "section", expert, None),
        P("section", None),
        P("section", None, None, expert),
        P("section", None, None, expert),
        P("section", None, expert, None),
        P(None, "section", None, None),
        P(None, "section", None, None),
        P(None, "section", None, None),
        P(None, "section", None, None),
    )
    return jax.shard_map(
        on_device,
        mesh=split,
        in_specs=placed,
        out_specs=(P("section", expert, None), P("section", expert, None)),
        check_vma=False,
    )
```

```python
import functools

import jax
import jax.numpy as jnp
from jax import lax
from jax.experimental import pallas as pl
from jax.experimental.pallas import tpu as pltpu
from jax.sharding import Mesh, PartitionSpec as P

CAP = 16
NX = 4
NZ = 2
EPSILON = 1e-06
BF = jnp.bfloat16
F32 = jnp.float32


def dot(a, b, contract=(1, 0)):
    dims = (((contract[0],), (contract[1],)), ((), ()))
    return lax.dot_general(a, b, dims, preferred_element_type=F32)


def to_x(block, distance):
    route = [(i, (i + distance) % NX) for i in range(NX)]
    return lax.ppermute(block, "x", route)


def to_other_z(block):
    return lax.ppermute(block, "zh", [(0, 1), (1, 0)])


def to_section(block, step):
    count = lax.axis_size("section")
    route = [(s, s + step) for s in range(count) if 0 <= s + step < count]
    return lax.ppermute(block, "section", route)


def routing_plans(ids, weights, zi):
    plans = ids.shape[0]
    matches = (ids == 0).astype(F32)
    mixing = jnp.sum(weights * matches, axis=-1).reshape(plans, NX, NZ, -1)
    member = jnp.sum(matches, axis=-1).reshape(plans, NX, NZ, -1)
    rows = member.shape[-1]
    swap = lambda a: jnp.where(zi == 0, a, a[:, :, ::-1])
    mixing = jnp.transpose(swap(mixing), (0, 2, 1, 3))
    member = jnp.transpose(swap(member), (0, 2, 1, 3))
    upto = (lax.broadcasted_iota(jnp.int32, (rows, rows), 0) <= lax.broadcasted_iota(jnp.int32, (rows, rows), 1)).astype(BF)
    order = dot(member.reshape(-1, rows).astype(BF), upto).reshape(member.shape)
    slot = jnp.where(member > 0, order, 0.0)
    wanted = jnp.arange(1, CAP + 1, dtype=jnp.int32).astype(F32)
    one_hot = (slot[..., None, :] == wanted[:, None]).astype(F32)
    spread = jnp.broadcast_to(mixing[..., None, :], one_hot.shape)
    slot_weight = jnp.sum((one_hot * spread).reshape(plans, -1, rows), axis=-1, keepdims=True)
    return one_hot.astype(BF), slot_weight


def after(value, *before):
    return lax.optimization_barrier((value,) + before)[0]


def two_words(column):
    high = lax.reduce_precision(column, 8, 7)
    low = column - high
    lane = lax.broadcasted_iota(jnp.int32, (column.shape[0], 128), 1)
    return jnp.where(lane == 0, high, jnp.where(lane == 1, low, 0.0)).astype(BF)


def kernel_call(kernel, outs, operands, smem_first=False, scratch=(), room=14, far=(), far_out=False):
    specs = [
        pl.BlockSpec(memory_space=pl.ANY if i in far else pltpu.VMEM) for i in range(len(operands))
    ]
    if smem_first:
        specs[0] = pl.BlockSpec(memory_space=pltpu.SMEM)
    return pl.pallas_call(
        kernel,
        out_shape=outs,
        in_specs=specs,
        out_specs=[pl.BlockSpec(memory_space=pl.ANY if far_out else pltpu.VMEM) for _ in outs],
        scratch_shapes=list(scratch),
        cost_estimate=pl.CostEstimate(flops=1000, bytes_accessed=1000, transcendentals=0),
        compiler_params=pltpu.CompilerParams(vmem_limit_bytes=room * 2**20),
    )(*operands)


def shape(dims, dtype):
    return jax.ShapeDtypeStruct(dims, dtype)


def column_block(index, width):
    return pl.ds(pl.multiple_of(lax.rem(index, NX) * width, 128), width)


def pack_kernel(where, hot, fwd, stash, cot, *rest):
    outs, (hat1, word1, packed, near_fwd, near_stash, near_cot, sems) = rest[:NX], rest[NX:]
    copies = [
        pltpu.make_async_copy(fwd, near_fwd, sems.at[0]),
        pltpu.make_async_copy(stash, near_stash, sems.at[1]),
        pltpu.make_async_copy(cot, near_cot, sems.at[2]),
    ]
    for copy in copies:
        copy.start()
    for copy in copies:
        copy.wait()
    fwd, stash, cot = near_fwd, near_stash, near_cot
    width = outs[0].shape[-1]
    x_fwd = dot(hot[0], fwd[...])
    x_bwd = dot(hot[2], stash[0])
    x_next = dot(hot[3], stash[1])
    g = dot(hot[2], cot[...])

    def inverse(x):
        return lax.rsqrt(jnp.mean(x * x, axis=-1, keepdims=True) + EPSILON)

    inv0, inv1 = inverse(x_bwd), inverse(x_next)
    packed[0] = (x_fwd * inverse(x_fwd)).astype(BF)
    packed[1] = (x_bwd * inv0).astype(BF)
    packed[2] = (g * inv0).astype(BF)
    hat1[...] = (x_next * inv1).astype(BF)
    word1[...] = jnp.broadcast_to(inv1, word1.shape)
    for d in range(NX):
        outs[d][...] = packed[:, :, column_block(where[0] + d, width)]


def pack_later_kernel(hot, fwd, cot, word1, out):
    depth = fwd.shape[-1]
    inv1 = word1[:, :1]
    out[0, :, :depth] = dot(hot[1], fwd[...]).astype(BF)
    out[1, :, :depth] = (dot(hot[3], cot[...]) * inv1).astype(BF)
    words = two_words(inv1)
    for i in range(2):
        out[i, :, depth:] = words


def weights_kernel(gate, up, down, *refs):
    outs, sems = refs[:NX], refs[NX]
    width, half = gate.shape[0] // NX, gate.shape[1]
    me = lax.axis_index("x")
    copies = []

    def move(source, target):
        copies.append(pltpu.make_async_copy(source, target, sems.at[len(copies)]))
        copies[-1].start()

    for d in (1, 3, 2, 0):
        at = pl.multiple_of(lax.rem(me + d, NX) * width, 128)
        move(gate.at[pl.ds(at, width), :], outs[d].at[:width, :half])
        move(up.at[pl.ds(at, width), :], outs[d].at[:width, half:])
        for j in range(width // (2 * half)):
            to = width + j * half
            across = pl.ds(pl.multiple_of(at + j * 2 * half, 128), 2 * half)
            move(down.at[:, across], outs[d].at[to : to + half, :])
    for copy in copies:
        copy.wait()


def down_blocks(weights):
    wide = weights.shape[1]
    half = wide // 2
    blocks = weights.shape[0] // (wide + half)
    for j in range(blocks):
        to = blocks * wide + j * half
        yield slice(j * wide, (j + 1) * wide), slice(to, to + half)


def times_down(hidden, weights, outs):
    for columns, lines in down_blocks(weights[0]):
        value = sum(dot(h, w[lines, :]) for h, w in zip(hidden, weights))
        put(outs, value, columns)


def times_down_back(x, weights):
    return sum(dot(x[:, columns], weights[lines, :], (1, 1)) for columns, lines in down_blocks(weights))


def split_kernel(where, own, other, own_hat, other_hat, *outs):
    width = own_hat.shape[-1] // NX
    for d in range(NX):
        at = column_block(where[0] + d, width)
        for side, (rows, hat) in enumerate(((own, own_hat), (other, other_hat))):
            lines = slice(side * CAP, (side + 1) * CAP)
            outs[d][:2, lines, :width] = rows[:, :, at]
            outs[d][:2, lines, width:] = rows[:, :, NX * width :]
            outs[d][2, lines, :width] = hat[:, at]
            outs[d][2, lines, width:] = rows[1, :, NX * width :]


def order_kernel(where, *refs):
    pieces, outs = refs[:NX], refs[NX:]
    for d in range(NX):
        at = pl.multiple_of(lax.rem(where[0] + NX - d, NX) * CAP, CAP)
        for side, out in enumerate(outs):
            out[:, pl.ds(at, CAP), :] = pieces[d][:, side * CAP : (side + 1) * CAP, :]


def both(own, other, index, width):
    return jnp.concatenate([own[index, :, :width], other[index, :, :width]], axis=0)


def gained(x, gain):
    return (x.astype(F32) * gain[...]).astype(BF)


def first_kernel(own, other, gain, *refs):
    weights, outs = refs[:NX], refs[NX:]
    width = gain.shape[-1]
    x_fwd = gained(both(own, other, 0, width), gain)
    x_bwd = gained(both(own, other, 1, width), gain)
    cot = both(own, other, 2, width)
    rows = x_fwd.shape[0]
    x = jnp.concatenate([x_fwd, x_bwd], axis=0)
    for w, out in zip(weights, outs):
        out[: 2 * rows, :] = dot(x, w[:width, :]).astype(out.dtype)
        hidden_cot = times_down_back(cot, w).astype(out.dtype)
        out[2 * rows :, : w.shape[1] // 2] = hidden_cot[: rows // 2]
        out[2 * rows :, w.shape[1] // 2 :] = hidden_cot[rows // 2 :]


def pre_next_kernel(own, other, gain, carry, straight, crossed, *refs):
    weights, outs = refs[:NX], refs[NX:]
    width, wide = gain.shape[-1], weights[0].shape[-1]
    count = straight.shape[0]
    x = both(own, other, 0, width).astype(F32)
    x = x + dot(carry[:, :count], straight[...]) + dot(carry[:, count:], crossed[...])
    squares = two_words(jnp.sum(x * x, axis=-1, keepdims=True))
    x = (x * gain[...]).astype(BF)
    for w, out in zip(weights, outs):
        out[:, :wide] = dot(x, w[:width, :]).astype(out.dtype)
        out[:, wide:] = squares.astype(out.dtype)


def cot_next_kernel(own, other, gain, carry, straight, crossed, *refs):
    weights, outs = refs[:NX], refs[NX:]
    width, count = straight.shape[-1], straight.shape[0]
    words = jnp.concatenate([own[1, :, width:], other[1, :, width:]], axis=0).astype(F32)
    inverse = words[:, :1] + words[:, 1:2]
    moved = dot(carry[:, :count], straight[...]) + dot(carry[:, count:], crossed[...])
    x = (both(own, other, 1, width).astype(F32) + inverse * moved).astype(BF)
    hat = gained(both(own, other, 2, width), gain)
    wide = weights[0].shape[-1]
    for w, out in zip(weights, outs):
        out[:, :wide] = dot(hat, w[:width, :]).astype(out.dtype)
        out[:, wide:] = times_down_back(x, w).astype(out.dtype)


def total(parts, rows=slice(None), columns=slice(None)):
    return sum(p[rows, columns].astype(F32) for p in parts)


def hidden_of(gate, up, mix):
    return (gate * jax.nn.sigmoid(gate) * up * mix).astype(BF)


def pair_of(hidden_cot, gate, up):
    sigma = jax.nn.sigmoid(gate)
    gate_cot = hidden_cot * up * sigma * (1.0 + gate * (1.0 - sigma))
    up_cot = hidden_cot * gate * sigma
    along = gate_cot * gate + up_cot * up
    return jnp.concatenate([gate_cot, up_cot, along], axis=1).astype(BF)


def middle_kernel(mix, *refs):
    parts, out = refs[:NX], refs[NX]
    count, half = out.shape[0], parts[0].shape[1] // 2
    pre = total(parts)
    hidden_cot = pre[2 * count :]
    hidden_cot = jnp.concatenate([hidden_cot[:, :half], hidden_cot[:, half:]], axis=0)
    out[:, :half] = hidden_of(pre[:count, :half], pre[:count, half:], mix[0])
    out[:, half:] = pair_of(
        hidden_cot * mix[2], pre[count : 2 * count, :half], pre[count : 2 * count, half:]
    )


def hidden_kernel(depth, mix, *refs):
    parts, out = refs[:NX], refs[NX]
    half = out.shape[1]
    pre = total(parts)
    words = pre[:, 2 * half :]
    scale = lax.rsqrt((words[:, :1] + words[:, 1:2]) / depth + EPSILON)
    out[...] = hidden_of(pre[:, :half] * scale, pre[:, half : 2 * half] * scale, mix[1])


def pair_kernel(mix, *refs):
    parts, out = refs[:NX], refs[NX]
    half = out.shape[1] // 3
    pre = total(parts)
    out[...] = pair_of(pre[:, 2 * half :] * mix[3], pre[:, :half], pre[:, half : 2 * half])


def put(outs, value, columns=slice(None)):
    at = 0
    for out in outs:
        out[:, columns] = value[at : at + out.shape[0]].astype(out.dtype)
        at += out.shape[0]


def cot_value(pairs, weights, gain, hat):
    width, wide = gain.shape[-1], weights[0].shape[-1]
    normed_cot = sum(dot(p[:, :wide], w[:width, :], (1, 1)) for p, w in zip(pairs, weights))
    along = sum(p[:, wide:].astype(F32) for p in pairs)
    along = jnp.sum(along, axis=-1, keepdims=True) / (NX * width)
    return normed_cot * gain[...] - hat.astype(F32) * along


def ends_kernel(own, other, gain, *refs):
    both_streams, weights, (out_fwd, out_cot) = refs[:NX], refs[NX : 2 * NX], refs[2 * NX :]
    half, width = weights[0].shape[-1] // 2, gain.shape[-1]
    times_down([p[:, :half] for p in both_streams], weights, [out_fwd])
    pairs = [p[:, half:] for p in both_streams]
    put([out_cot], cot_value(pairs, weights, gain, both(own, other, 1, width)))


def ffn_kernel(*refs):
    hidden, weights, outs = refs[:NX], refs[NX : 2 * NX], refs[2 * NX :]
    times_down([h[...] for h in hidden], weights, outs)


def cot_out_kernel(own, other, gain, *refs):
    pairs, weights, outs = refs[:NX], refs[NX : 2 * NX], refs[2 * NX :]
    pairs = [p[...] for p in pairs]
    put(outs, cot_value(pairs, weights, gain, both(own, other, 2, gain.shape[-1])))


def final_kernel(where, base, hot0, hot1, *refs):
    pieces, out = refs[:NX], refs[NX]
    width = pieces[0].shape[-1]
    for d in range(NX):
        at = column_block(where[0] + NX - d, width)
        rows = base[:, at].astype(F32) + dot(hot0[...], pieces[d][0])
        rows = rows.astype(BF).astype(F32) + dot(hot1[...], pieces[d][1], (0, 0))
        out[:, at] = rows.astype(BF)


def back_x(deltas, xi):
    pieces = []
    for d in range(NX):
        part = lax.dynamic_slice_in_dim(deltas, ((xi + d) % NX) * CAP, CAP, 1)
        pieces.append(part if d == 0 else to_x(part, d))
    return pieces


def gather_x(block):
    return [block] + [to_x(block, d) for d in range(1, NX)]


def sum_parts(parts):
    return [parts[0]] + [to_x(parts[d], -d) for d in range(1, NX)]


def on_device(
    forward_in,
    entering,
    cotangent_in,
    cot_entering,
    stash,
    norm_gain,
    w_gate,
    w_up,
    w_down,
    ids_fwd,
    route_fwd,
    ids_bwd,
    route_bwd,
):
    section = lax.axis_index("section")
    last = lax.axis_size("section") - 1
    xi = lax.axis_index("x")
    zi = lax.axis_index("zh")
    depth = stash.shape[-1]
    width = depth // NX
    half = w_gate.shape[-1]
    rows = NZ * NX * CAP

    ids = jnp.concatenate([ids_fwd[:, 0], ids_bwd[:, 0]], axis=0)
    routes = jnp.concatenate([route_fwd[:, 0], route_bwd[:, 0]], axis=0)
    hot, mix = routing_plans(ids, routes, zi)
    own = lax.dynamic_index_in_dim(hot[:, 0], xi, 1, keepdims=False)
    flat = hot.reshape(4, rows, -1)

    where = xi.astype(jnp.int32).reshape(1)

    wide = [shape((3, CAP, width), BF)] * NX
    *first, hat1, word1 = kernel_call(
        pack_kernel,
        wide + [shape((CAP, depth), BF), shape((CAP, 128), F32)],
        [where, own, forward_in[0], stash[:, 0], cotangent_in[0]],
        smem_first=True,
        scratch=[
            pltpu.VMEM((3, CAP, depth), BF),
            pltpu.VMEM(forward_in.shape[1:], BF),
            pltpu.VMEM((2,) + forward_in.shape[1:], BF),
            pltpu.VMEM(forward_in.shape[1:], BF),
            pltpu.SemaphoreType.DMA((3,)),
        ],
        room=58,
        far=(2, 3, 4),
    )
    first = [first[0]] + [to_x(first[d], d) for d in range(1, NX)]

    weights = kernel_call(
        weights_kernel,
        [shape((width + width // 2, 2 * half), BF)] * NX,
        [after(w_gate[0, 0], hat1), w_up[0, 0], w_down[0, 0]],
        scratch=[pltpu.SemaphoreType.DMA((NX * (2 + width // (2 * half)),))],
        room=58,
        far=(0, 1, 2),
    )
    first[0] = after(first[0], weights[0])
    weights = [weights[0]] + [to_x(weights[d], d) for d in range(1, NX)]

    def in_order(pieces, sides, room=14):
        count, _, columns = pieces[0].shape
        outs = [shape((count, NX * CAP, columns), BF)] * sides
        return kernel_call(order_kernel, outs, [where] + pieces, smem_first=True, room=room)

    first_own = in_order(first, 1, 44)[0]
    first_other = to_other_z(first_own)

    gain = lax.dynamic_slice_in_dim(norm_gain, xi * width, width, 1)

    turned = jnp.swapaxes(flat, 1, 2)
    moved_fwd = to_section(jnp.concatenate([forward_in[0], turned[0]], axis=1), 1)
    moved_cot = to_section(jnp.concatenate([cotangent_in[0], turned[2]], axis=1), -1)
    base_fwd = jnp.where(section == 0, entering[0], moved_fwd[:, :depth])
    base_cot = jnp.where(section == last, cot_entering[0], moved_cot[:, :depth])
    hot_fwd, hot_cot = moved_fwd[:, depth:], moved_cot[:, depth:]
    later = kernel_call(
        pack_later_kernel,
        [shape((2, CAP, depth + 128), BF)],
        [own, base_fwd, base_cot, word1],
    )[0]
    later_far = to_other_z(after(later, first_other))

    def cross_x(hat1_far, *before):
        pieces = kernel_call(
            split_kernel,
            [shape((3, 2 * CAP, width + 128), BF)] * NX,
            [where, after(later, *before), later_far, hat1, hat1_far],
            smem_first=True,
        )
        return in_order([pieces[0]] + [to_x(pieces[d], d) for d in range(1, NX)], 2)

    group = jnp.arange(rows) // CAP
    same = (group[:, None] == group[None, :]).astype(F32)

    def carry(plan, before):
        move = (dot(flat[plan], before) * same).astype(BF)
        return jnp.concatenate([move, jnp.roll(move, NX * CAP, axis=1)], axis=1)

    carry_fwd = carry(1, hot_fwd)
    carry_cot = carry(3, hot_cot)
    own_fwd0 = lax.dynamic_slice_in_dim(hot_fwd, xi * CAP, CAP, 1)
    own_cot0 = lax.dynamic_slice_in_dim(hot_cot, xi * CAP, CAP, 1)

    def parts_of(kernel, operands, columns, count):
        outs = [shape((count, columns), F32)] + [shape((count, columns), BF)] * (NX - 1)
        return kernel_call(kernel, outs, operands)

    whole = [shape((rows, width), BF)]
    halves = [shape((NX * CAP, width), BF)] * 2

    parts = sum_parts(
        parts_of(
            first_kernel,
            [after(first_own, later_far), first_other, gain] + weights,
            2 * half,
            2 * rows + rows // 2,
        )
    )
    hat1_far = to_other_z(after(hat1, parts[0]))
    middle = [shape((rows, 4 * half), BF)]
    middle = kernel_call(middle_kernel, middle, [mix] + parts)[0]
    fwd0, cot0 = kernel_call(
        ends_kernel, whole * 2, [after(first_own, hat1_far, carry_fwd, carry_cot), first_other, gain] + gather_x(middle) + weights
    )
    cot_straight = to_section(cot0, -1)
    cot_crossed = to_other_z(cot_straight)
    fwd_straight = to_section(fwd0, 1)
    fwd_crossed = to_other_z(fwd_straight)

    later_own, later_other = cross_x(hat1_far, cot0)
    sums1 = sum_parts(
        parts_of(
            cot_next_kernel,
            [later_own, later_other, gain, carry_cot, cot_straight, cot_crossed] + weights,
            3 * half,
            rows,
        )
    )
    pair1 = kernel_call(pair_kernel, [shape((rows, 3 * half), BF)], [mix] + sums1)[0]
    cot1 = kernel_call(
        cot_out_kernel, halves, [later_own, later_other, gain] + gather_x(pair1) + weights
    )
    next_pre = sum_parts(
        parts_of(
            pre_next_kernel,
            [later_own, later_other, gain, after(carry_fwd, cot1[0]), fwd_straight, fwd_crossed]
            + weights,
            3 * half,
            rows,
        )
    )
    hidden_kind = [shape((rows, half), BF)]
    hidden1 = kernel_call(functools.partial(hidden_kernel, depth), hidden_kind, [mix] + next_pre)[0]
    fwd1 = kernel_call(ffn_kernel, halves, gather_x(hidden1) + weights)

    def add_half(a, b):
        return (a.astype(F32) + b.astype(F32)).astype(BF)

    def finish(base, hot0, hot1, straight, crossed, now):
        count = NX * CAP
        before = add_half(straight[:count], crossed[count:])
        pieces = back_x(jnp.stack([before, add_half(now[0], to_other_z(now[1]))]), xi)
        out = [shape(base.shape, BF)]
        return kernel_call(final_kernel, out, [where, base, hot0, hot1] + pieces, smem_first=True)[0]

    cot_end = finish(base_cot, own_cot0, own[3], cot_straight, cot_crossed, cot1)
    fwd_end = finish(base_fwd, own_fwd0, own[1], fwd_straight, fwd_crossed, fwd1)
    return (fwd_end[None], cot_end[None])


def solution(mesh):
    split = Mesh(mesh.devices.reshape(-1, NX, NZ), ("section", "x", "zh"))
    expert = ("x", "zh")
    placed = (
        P("section", expert, None),
        P(None, expert, None),
        P("section", expert, None),
        P(None, expert, None),
        P(None, "section", expert, None),
        P("section", None),
        P("section", None, None, expert),
        P("section", None, None, expert),
        P("section", None, expert, None),
        P(None, "section", None, None),
        P(None, "section", None, None),
        P(None, "section", None, None),
        P(None, "section", None, None),
    )
    return jax.shard_map(
        on_device,
        mesh=split,
        in_specs=placed,
        out_specs=(P("section", expert, None), P("section", expert, None)),
        check_vma=False,
    )
```

```python
import functools

import jax
import jax.numpy as jnp
from jax import lax
from jax.experimental import pallas as pl
from jax.experimental.pallas import tpu as pltpu
from jax.sharding import Mesh, PartitionSpec as P

CAP = 16
NX = 4
NZ = 2
EPSILON = 1e-06
BF = jnp.bfloat16
F32 = jnp.float32


def dot(a, b, contract=(1, 0)):
    dims = (((contract[0],), (contract[1],)), ((), ()))
    return lax.dot_general(a, b, dims, preferred_element_type=F32)


def to_x(block, distance):
    route = [(i, (i + distance) % NX) for i in range(NX)]
    return lax.ppermute(block, "x", route)


def to_other_z(block):
    return lax.ppermute(block, "zh", [(0, 1), (1, 0)])


def to_section(block, step):
    count = lax.axis_size("section")
    route = [(s, s + step) for s in range(count) if 0 <= s + step < count]
    return lax.ppermute(block, "section", route)


def routing_plans(ids, weights, zi):
    plans = ids.shape[0]
    matches = (ids == 0).astype(F32)
    mixing = jnp.sum(weights * matches, axis=-1).reshape(plans, NX, NZ, -1)
    member = jnp.sum(matches, axis=-1).reshape(plans, NX, NZ, -1)
    rows = member.shape[-1]
    swap = lambda a: jnp.where(zi == 0, a, a[:, :, ::-1])
    mixing = jnp.transpose(swap(mixing), (0, 2, 1, 3))
    member = jnp.transpose(swap(member), (0, 2, 1, 3))
    upto = (lax.broadcasted_iota(jnp.int32, (rows, rows), 0) <= lax.broadcasted_iota(jnp.int32, (rows, rows), 1)).astype(BF)
    order = dot(member.reshape(-1, rows).astype(BF), upto).reshape(member.shape)
    slot = jnp.where(member > 0, order, 0.0)
    wanted = jnp.arange(1, CAP + 1, dtype=jnp.int32).astype(F32)
    one_hot = (slot[..., None, :] == wanted[:, None]).astype(F32)
    spread = jnp.broadcast_to(mixing[..., None, :], one_hot.shape)
    slot_weight = jnp.sum((one_hot * spread).reshape(plans, -1, rows), axis=-1, keepdims=True)
    return one_hot.astype(BF), slot_weight


def after(value, *before):
    return lax.optimization_barrier((value,) + before)[0]


def two_words(column):
    high = lax.reduce_precision(column, 8, 7)
    low = column - high
    lane = lax.broadcasted_iota(jnp.int32, (column.shape[0], 128), 1)
    return jnp.where(lane == 0, high, jnp.where(lane == 1, low, 0.0)).astype(BF)


def kernel_call(kernel, outs, operands, smem_first=False, scratch=(), room=14, far=(), far_out=False):
    specs = [
        pl.BlockSpec(memory_space=pl.ANY if i in far else pltpu.VMEM) for i in range(len(operands))
    ]
    if smem_first:
        specs[0] = pl.BlockSpec(memory_space=pltpu.SMEM)
    return pl.pallas_call(
        kernel,
        out_shape=outs,
        in_specs=specs,
        out_specs=[pl.BlockSpec(memory_space=pl.ANY if far_out else pltpu.VMEM) for _ in outs],
        scratch_shapes=list(scratch),
        cost_estimate=pl.CostEstimate(flops=1000, bytes_accessed=1000, transcendentals=0),
        compiler_params=pltpu.CompilerParams(vmem_limit_bytes=room * 2**20),
    )(*operands)


def shape(dims, dtype):
    return jax.ShapeDtypeStruct(dims, dtype)


def column_block(index, width):
    return pl.ds(pl.multiple_of(lax.rem(index, NX) * width, 128), width)


def pack_kernel(where, hot, fwd, stash, cot, *rest):
    outs, (hat1, word1, packed, near_fwd, near_stash, near_cot, sems) = rest[:NX], rest[NX:]
    copies = [
        pltpu.make_async_copy(fwd, near_fwd, sems.at[0]),
        pltpu.make_async_copy(stash, near_stash, sems.at[1]),
        pltpu.make_async_copy(cot, near_cot, sems.at[2]),
    ]
    for copy in copies:
        copy.start()
    for copy in copies:
        copy.wait()
    fwd, stash, cot = near_fwd, near_stash, near_cot
    width = outs[0].shape[-1]
    x_fwd = dot(hot[0], fwd[...])
    x_bwd = dot(hot[2], stash[0])
    x_next = dot(hot[3], stash[1])
    g = dot(hot[2], cot[...])

    def inverse(x):
        return lax.rsqrt(jnp.mean(x * x, axis=-1, keepdims=True) + EPSILON)

    inv0, inv1 = inverse(x_bwd), inverse(x_next)
    packed[0] = (x_fwd * inverse(x_fwd)).astype(BF)
    packed[1] = (x_bwd * inv0).astype(BF)
    packed[2] = (g * inv0).astype(BF)
    hat1[...] = (x_next * inv1).astype(BF)
    word1[...] = jnp.broadcast_to(inv1, word1.shape)
    for d in range(NX):
        outs[d][...] = packed[:, :, column_block(where[0] + d, width)]


def pack_later_kernel(hot, fwd, cot, word1, out):
    depth = fwd.shape[-1]
    inv1 = word1[:, :1]
    out[0, :, :depth] = dot(hot[1], fwd[...]).astype(BF)
    out[1, :, :depth] = (dot(hot[3], cot[...]) * inv1).astype(BF)
    words = two_words(inv1)
    for i in range(2):
        out[i, :, depth:] = words


def weights_kernel(gate, up, down, *refs):
    outs, sems = refs[:NX], refs[NX]
    width, half = gate.shape[0] // NX, gate.shape[1]
    me = lax.axis_index("x")
    copies = []

    def move(source, target):
        copies.append(pltpu.make_async_copy(source, target, sems.at[len(copies)]))
        copies[-1].start()

    for d in (1, 3, 2, 0):
        at = pl.multiple_of(lax.rem(me + d, NX) * width, 128)
        move(gate.at[pl.ds(at, width), :], outs[d].at[:width, :half])
        move(up.at[pl.ds(at, width), :], outs[d].at[:width, half:])
        for j in range(width // (2 * half)):
            to = width + j * half
            across = pl.ds(pl.multiple_of(at + j * 2 * half, 128), 2 * half)
            move(down.at[:, across], outs[d].at[to : to + half, :])
    for copy in copies:
        copy.wait()


def down_blocks(weights):
    wide = weights.shape[1]
    half = wide // 2
    blocks = weights.shape[0] // (wide + half)
    for j in range(blocks):
        to = blocks * wide + j * half
        yield slice(j * wide, (j + 1) * wide), slice(to, to + half)


def times_down(hidden, weights, outs):
    for columns, lines in down_blocks(weights[0]):
        value = sum(dot(h, w[lines, :]) for h, w in zip(hidden, weights))
        put(outs, value, columns)


def times_down_back(x, weights):
    return sum(dot(x[:, columns], weights[lines, :], (1, 1)) for columns, lines in down_blocks(weights))


def split_kernel(where, own, other, own_hat, other_hat, *outs):
    width = own_hat.shape[-1] // NX
    for d in range(NX):
        at = column_block(where[0] + d, width)
        for side, (rows, hat) in enumerate(((own, own_hat), (other, other_hat))):
            lines = slice(side * CAP, (side + 1) * CAP)
            outs[d][:2, lines, :width] = rows[:, :, at]
            outs[d][:2, lines, width:] = rows[:, :, NX * width :]
            outs[d][2, lines, :width] = hat[:, at]
            outs[d][2, lines, width:] = rows[1, :, NX * width :]


def order_kernel(where, *refs):
    pieces, outs = refs[:NX], refs[NX:]
    for d in range(NX):
        at = pl.multiple_of(lax.rem(where[0] + NX - d, NX) * CAP, CAP)
        for side, out in enumerate(outs):
            out[:, pl.ds(at, CAP), :] = pieces[d][:, side * CAP : (side + 1) * CAP, :]


def both(own, other, index, width):
    return jnp.concatenate([own[index, :, :width], other[index, :, :width]], axis=0)


def gained(x, gain):
    return (x.astype(F32) * gain[...]).astype(BF)


def first_kernel(own, other, gain, *refs):
    weights, outs = refs[:NX], refs[NX:]
    width = gain.shape[-1]
    x_fwd = gained(both(own, other, 0, width), gain)
    x_bwd = gained(both(own, other, 1, width), gain)
    cot = both(own, other, 2, width)
    rows = x_fwd.shape[0]
    x = jnp.concatenate([x_fwd, x_bwd], axis=0)
    for w, out in zip(weights, outs):
        out[: 2 * rows, :] = dot(x, w[:width, :]).astype(out.dtype)
        hidden_cot = times_down_back(cot, w).astype(out.dtype)
        out[2 * rows :, : w.shape[1] // 2] = hidden_cot[: rows // 2]
        out[2 * rows :, w.shape[1] // 2 :] = hidden_cot[rows // 2 :]


def pre_next_kernel(own, other, gain, carry, straight, crossed, *refs):
    weights, outs = refs[:NX], refs[NX:]
    width, wide = gain.shape[-1], weights[0].shape[-1]
    count = straight.shape[0]
    x = both(own, other, 0, width).astype(F32)
    x = x + dot(carry[:, :count], straight[...]) + dot(carry[:, count:], crossed[...])
    squares = two_words(jnp.sum(x * x, axis=-1, keepdims=True))
    x = (x * gain[...]).astype(BF)
    for w, out in zip(weights, outs):
        out[:, :wide] = dot(x, w[:width, :]).astype(out.dtype)
        out[:, wide:] = squares.astype(out.dtype)


def cot_next_kernel(own, other, gain, carry, straight, crossed, *refs):
    weights, outs = refs[:NX], refs[NX:]
    width, count = straight.shape[-1], straight.shape[0]
    words = jnp.concatenate([own[1, :, width:], other[1, :, width:]], axis=0).astype(F32)
    inverse = words[:, :1] + words[:, 1:2]
    moved = dot(carry[:, :count], straight[...]) + dot(carry[:, count:], crossed[...])
    x = (both(own, other, 1, width).astype(F32) + inverse * moved).astype(BF)
    hat = gained(both(own, other, 2, width), gain)
    wide = weights[0].shape[-1]
    for w, out in zip(weights, outs):
        out[:, :wide] = dot(hat, w[:width, :]).astype(out.dtype)
        out[:, wide:] = times_down_back(x, w).astype(out.dtype)


def total(parts, rows=slice(None), columns=slice(None)):
    return sum(p[rows, columns].astype(F32) for p in parts)


def hidden_of(gate, up, mix):
    return (gate * jax.nn.sigmoid(gate) * up * mix).astype(BF)


def pair_of(hidden_cot, gate, up):
    sigma = jax.nn.sigmoid(gate)
    gate_cot = hidden_cot * up * sigma * (1.0 + gate * (1.0 - sigma))
    up_cot = hidden_cot * gate * sigma
    along = gate_cot * gate + up_cot * up
    return jnp.concatenate([gate_cot, up_cot, along], axis=1).astype(BF)


def middle_kernel(mix, *refs):
    parts, out = refs[:NX], refs[NX]
    count, half = out.shape[0], parts[0].shape[1] // 2
    pre = total(parts)
    hidden_cot = pre[2 * count :]
    hidden_cot = jnp.concatenate([hidden_cot[:, :half], hidden_cot[:, half:]], axis=0)
    out[:, :half] = hidden_of(pre[:count, :half], pre[:count, half:], mix[0])
    out[:, half:] = pair_of(
        hidden_cot * mix[2], pre[count : 2 * count, :half], pre[count : 2 * count, half:]
    )


def hidden_kernel(depth, mix, *refs):
    parts, out = refs[:NX], refs[NX]
    half = out.shape[1]
    pre = total(parts)
    words = pre[:, 2 * half :]
    scale = lax.rsqrt((words[:, :1] + words[:, 1:2]) / depth + EPSILON)
    out[...] = hidden_of(pre[:, :half] * scale, pre[:, half : 2 * half] * scale, mix[1])


def pair_kernel(mix, *refs):
    parts, out = refs[:NX], refs[NX]
    half = out.shape[1] // 3
    pre = total(parts)
    out[...] = pair_of(pre[:, 2 * half :] * mix[3], pre[:, :half], pre[:, half : 2 * half])


def put(outs, value, columns=slice(None)):
    at = 0
    for out in outs:
        out[:, columns] = value[at : at + out.shape[0]].astype(out.dtype)
        at += out.shape[0]


def cot_value(pairs, weights, gain, hat):
    width, wide = gain.shape[-1], weights[0].shape[-1]
    normed_cot = sum(dot(p[:, :wide], w[:width, :], (1, 1)) for p, w in zip(pairs, weights))
    along = sum(p[:, wide:].astype(F32) for p in pairs)
    along = jnp.sum(along, axis=-1, keepdims=True) / (NX * width)
    return normed_cot * gain[...] - hat.astype(F32) * along


def ends_kernel(own, other, gain, *refs):
    both_streams, weights, (out_fwd, out_cot) = refs[:NX], refs[NX : 2 * NX], refs[2 * NX :]
    half, width = weights[0].shape[-1] // 2, gain.shape[-1]
    times_down([p[:, :half] for p in both_streams], weights, [out_fwd])
    pairs = [p[:, half:] for p in both_streams]
    put([out_cot], cot_value(pairs, weights, gain, both(own, other, 1, width)))


def ffn_kernel(*refs):
    hidden, weights, outs = refs[:NX], refs[NX : 2 * NX], refs[2 * NX :]
    times_down([h[...] for h in hidden], weights, outs)


def cot_out_kernel(own, other, gain, *refs):
    pairs, weights, outs = refs[:NX], refs[NX : 2 * NX], refs[2 * NX :]
    pairs = [p[...] for p in pairs]
    put(outs, cot_value(pairs, weights, gain, both(own, other, 2, gain.shape[-1])))


def final_kernel(where, base, hot0, hot1, *refs):
    pieces, out = refs[:NX], refs[NX]
    width = pieces[0].shape[-1]
    for d in range(NX):
        at = column_block(where[0] + NX - d, width)
        rows = base[:, at].astype(F32) + dot(hot0[...], pieces[d][0])
        rows = rows.astype(BF).astype(F32) + dot(hot1[...], pieces[d][1], (0, 0))
        out[:, at] = rows.astype(BF)


def back_x(deltas, xi):
    pieces = []
    for d in range(NX):
        part = lax.dynamic_slice_in_dim(deltas, ((xi + d) % NX) * CAP, CAP, 1)
        pieces.append(part if d == 0 else to_x(part, d))
    return pieces


def gather_x(block):
    return [block] + [to_x(block, d) for d in range(1, NX)]


def sum_parts(parts):
    return [parts[0]] + [to_x(parts[d], -d) for d in range(1, NX)]


def on_device(
    forward_in,
    entering,
    cotangent_in,
    cot_entering,
    stash,
    norm_gain,
    w_gate,
    w_up,
    w_down,
    ids_fwd,
    route_fwd,
    ids_bwd,
    route_bwd,
):
    section = lax.axis_index("section")
    last = lax.axis_size("section") - 1
    xi = lax.axis_index("x")
    zi = lax.axis_index("zh")
    depth = stash.shape[-1]
    width = depth // NX
    half = w_gate.shape[-1]
    rows = NZ * NX * CAP

    ids = jnp.concatenate([ids_fwd[:, 0], ids_bwd[:, 0]], axis=0)
    routes = jnp.concatenate([route_fwd[:, 0], route_bwd[:, 0]], axis=0)
    hot, mix = routing_plans(ids, routes, zi)
    own = lax.dynamic_index_in_dim(hot[:, 0], xi, 1, keepdims=False)
    flat = hot.reshape(4, rows, -1)

    where = xi.astype(jnp.int32).reshape(1)

    wide = [shape((3, CAP, width), BF)] * NX
    *first, hat1, word1 = kernel_call(
        pack_kernel,
        wide + [shape((CAP, depth), BF), shape((CAP, 128), F32)],
        [where, own, forward_in[0], stash[:, 0], cotangent_in[0]],
        smem_first=True,
        scratch=[
            pltpu.VMEM((3, CAP, depth), BF),
            pltpu.VMEM(forward_in.shape[1:], BF),
            pltpu.VMEM((2,) + forward_in.shape[1:], BF),
            pltpu.VMEM(forward_in.shape[1:], BF),
            pltpu.SemaphoreType.DMA((3,)),
        ],
        room=58,
        far=(2, 3, 4),
    )
    first = [first[0]] + [to_x(first[d], d) for d in range(1, NX)]

    weights = kernel_call(
        weights_kernel,
        [shape((width + width // 2, 2 * half), BF)] * NX,
        [after(w_gate[0, 0], hat1), w_up[0, 0], w_down[0, 0]],
        scratch=[pltpu.SemaphoreType.DMA((NX * (2 + width // (2 * half)),))],
        room=58,
        far=(0, 1, 2),
    )
    first[0] = after(first[0], weights[0])
    weights = [weights[0]] + [to_x(weights[d], d) for d in range(1, NX)]

    def in_order(pieces, sides, room=14):
        count, _, columns = pieces[0].shape
        outs = [shape((count, NX * CAP, columns), BF)] * sides
        return kernel_call(order_kernel, outs, [where] + pieces, smem_first=True, room=room)

    first_own = in_order(first, 1, 44)[0]
    first_other = to_other_z(first_own)

    gain = lax.dynamic_slice_in_dim(norm_gain, xi * width, width, 1)

    turned = jnp.swapaxes(flat, 1, 2)
    turned = after(turned, weights[0], first[1])
    moved_fwd = to_section(jnp.concatenate([forward_in[0], turned[0]], axis=1), 1)
    moved_cot = to_section(jnp.concatenate([cotangent_in[0], turned[2]], axis=1), -1)
    base_fwd = jnp.where(section == 0, entering[0], moved_fwd[:, :depth])
    base_cot = jnp.where(section == last, cot_entering[0], moved_cot[:, :depth])
    hot_fwd, hot_cot = moved_fwd[:, depth:], moved_cot[:, depth:]
    later = kernel_call(
        pack_later_kernel,
        [shape((2, CAP, depth + 128), BF)],
        [own, base_fwd, base_cot, word1],
    )[0]
    later_far = to_other_z(after(later, first_other))

    def cross_x(hat1_far, *before):
        pieces = kernel_call(
            split_kernel,
            [shape((3, 2 * CAP, width + 128), BF)] * NX,
            [where, after(later, *before), later_far, hat1, hat1_far],
            smem_first=True,
        )
        return in_order([pieces[0]] + [to_x(pieces[d], d) for d in range(1, NX)], 2)

    group = jnp.arange(rows) // CAP
    same = (group[:, None] == group[None, :]).astype(F32)

    def carry(plan, before):
        move = (dot(flat[plan], before) * same).astype(BF)
        return jnp.concatenate([move, jnp.roll(move, NX * CAP, axis=1)], axis=1)

    carry_fwd = carry(1, hot_fwd)
    carry_cot = carry(3, hot_cot)
    own_fwd0 = lax.dynamic_slice_in_dim(hot_fwd, xi * CAP, CAP, 1)
    own_cot0 = lax.dynamic_slice_in_dim(hot_cot, xi * CAP, CAP, 1)

    def parts_of(kernel, operands, columns, count):
        outs = [shape((count, columns), F32)] + [shape((count, columns), BF)] * (NX - 1)
        return kernel_call(kernel, outs, operands)

    whole = [shape((rows, width), BF)]
    halves = [shape((NX * CAP, width), BF)] * 2

    parts = sum_parts(
        parts_of(
            first_kernel,
            [after(first_own, later_far), first_other, gain] + weights,
            2 * half,
            2 * rows + rows // 2,
        )
    )
    hat1_far = to_other_z(after(hat1, parts[0]))
    middle = [shape((rows, 4 * half), BF)]
    middle = kernel_call(middle_kernel, middle, [mix] + parts)[0]
    fwd0, cot0 = kernel_call(
        ends_kernel, whole * 2, [after(first_own, hat1_far, carry_fwd, carry_cot), first_other, gain] + gather_x(middle) + weights
    )
    cot_straight = to_section(cot0, -1)
    cot_crossed = to_other_z(cot_straight)
    fwd_straight = to_section(fwd0, 1)
    fwd_crossed = to_other_z(fwd_straight)

    later_own, later_other = cross_x(hat1_far, cot0)
    sums1 = sum_parts(
        parts_of(
            cot_next_kernel,
            [later_own, later_other, gain, carry_cot, cot_straight, cot_crossed] + weights,
            3 * half,
            rows,
        )
    )
    pair1 = kernel_call(pair_kernel, [shape((rows, 3 * half), BF)], [mix] + sums1)[0]
    cot1 = kernel_call(
        cot_out_kernel, halves, [later_own, later_other, gain] + gather_x(pair1) + weights
    )
    next_pre = sum_parts(
        parts_of(
            pre_next_kernel,
            [later_own, later_other, gain, after(carry_fwd, cot1[0]), fwd_straight, fwd_crossed]
            + weights,
            3 * half,
            rows,
        )
    )
    hidden_kind = [shape((rows, half), BF)]
    hidden1 = kernel_call(functools.partial(hidden_kernel, depth), hidden_kind, [mix] + next_pre)[0]
    fwd1 = kernel_call(ffn_kernel, halves, gather_x(hidden1) + weights)

    def add_half(a, b):
        return (a.astype(F32) + b.astype(F32)).astype(BF)

    def finish(base, hot0, hot1, straight, crossed, now):
        count = NX * CAP
        before = add_half(straight[:count], crossed[count:])
        pieces = back_x(jnp.stack([before, add_half(now[0], to_other_z(now[1]))]), xi)
        out = [shape(base.shape, BF)]
        return kernel_call(final_kernel, out, [where, base, hot0, hot1] + pieces, smem_first=True)[0]

    cot_end = finish(base_cot, own_cot0, own[3], cot_straight, cot_crossed, cot1)
    fwd_end = finish(base_fwd, own_fwd0, own[1], fwd_straight, fwd_crossed, fwd1)
    return (fwd_end[None], cot_end[None])


def solution(mesh):
    split = Mesh(mesh.devices.reshape(-1, NX, NZ), ("section", "x", "zh"))
    expert = ("x", "zh")
    placed = (
        P("section", expert, None),
        P(None, expert, None),
        P("section", expert, None),
        P(None, expert, None),
        P(None, "section", expert, None),
        P("section", None),
        P("section", None, None, expert),
        P("section", None, None, expert),
        P("section", None, expert, None),
        P(None, "section", None, None),
        P(None, "section", None, None),
        P(None, "section", None, None),
        P(None, "section", None, None),
    )
    return jax.shard_map(
        on_device,
        mesh=split,
        in_specs=placed,
        out_specs=(P("section", expert, None), P("section", expert, None)),
        check_vma=False,
    )
```
